512 devices in a mesh: cfg: 2 (over core), head: 8 (over z), kv: 32 (over x, y).
Axes of the slice: x: 4, y: 8, z: 8, core: 2. Of those that a mesh axis runs over, the one named last changes fastest.
Arguments:
- queries: bfloat16 [32, 128, 5120], P(('cfg', 'head'), 'kv'), parts along dimension 0, may hold values from -20 to 20
- keys: bfloat16 [128, 128, 5120], P(('cfg', 'kv'), 'head'), parts along dimension 0, may hold values from -20 to 20
- values: bfloat16 [128, 128, 5120], P(('cfg', 'kv'), 'head'), parts along dimension 0, may hold values from -6 to 6
- mask_cols: int32 [16, 32], replicated, may hold values from 0 to 63, as said below
- mask_counts: int32 [16], replicated, may hold values from 16 to 32
Outputs:
- attended: bfloat16 [32, 128, 5120], P(('cfg', 'head'), 'kv'), parts along dimension 0
The draws below stay inside these ranges and needn't reach their ends.
There are 2 independent parts, one for each index of `cfg`. The reference program is written for one: setup_inputs(seed, part) draws one part's arguments, and reference() takes and returns one part's arrays. A program takes and returns all parts, laid end to end along the dimension named above; an argument that names none is the same for every part. Nothing has to cross between parts.
Inputs may be any that keep to these rules, and one draw needn't show every extreme that they name: `mask_cols`: within a row the entries are distinct key blocks.
All inputs are finite; a program needn't handle non-finite values.
Results may differ from the reference program's by a relative error of at most 0.0055.
Values may be sent and summed in bfloat16 or wider, within the bound.
No kernel may reach another device: no remote copies, remote signals or barrier semaphores. Data moves between devices by JAX's collectives and lax.ppermute only.
A program may use at most 64 MiB of HBM per device.

```python
import jax
import jax.numpy as jnp
from jax import lax

DH = 128
D = 5120
BLOCK = 128
KB_DEV = 2
QB = 16
LIST = 32
FRAMES = 8
NKB = 64


def draw_queries(key, part):
    key = jax.random.fold_in(key, 11)
    drawn = jnp.clip(jax.random.normal(key, (QB, BLOCK, D), jnp.float32), -4.0, 4.0)
    return drawn.astype(jnp.bfloat16)


def draw_keys(key, part):
    key = jax.random.fold_in(key, 12)
    drawn = jnp.clip(jax.random.normal(key, (NKB, BLOCK, D), jnp.float32), -4.0, 4.0)
    return drawn.astype(jnp.bfloat16)


def draw_mask_cols(key, part):
    key = jax.random.fold_in(key, 21)
    jitter_key, order_key = jax.random.split(key)
    frame_blocks = NKB // FRAMES
    place = jnp.arange(QB, dtype=jnp.int32) * (NKB // QB)
    blocks = jnp.arange(NKB, dtype=jnp.int32)
    frame_gap = jnp.abs(blocks[None, :] // frame_blocks - place[:, None] // frame_blocks)
    spot_gap = jnp.abs(blocks[None, :] % frame_blocks - place[:, None] % frame_blocks)
    jitter = jax.random.randint(jitter_key, (QB, NKB), 0, 4)
    priority = spot_gap * (1 + frame_gap) + jitter + 1
    priority = jnp.where(blocks[None, :] == place[:, None], 0, priority)
    tiebreak = jax.random.permutation(order_key, NKB).astype(jnp.int32)
    score = (4096 - priority) * 4096 + tiebreak[None, :]
    _, chosen = lax.top_k(score, LIST)
    return chosen.astype(jnp.int32)


def draw_mask_counts(key, part):
    key = jax.random.fold_in(key, 22)
    counts = jax.random.randint(key, (QB,), LIST // 2, LIST + 1)
    return counts.at[0].set(LIST).astype(jnp.int32)


def steps_of(own_key, dims, pieces, low, top_value):
    def one(dim, shards_of):
        heights = jax.random.uniform(jax.random.fold_in(jax.random.fold_in(own_key, 6), dim), (shards_of,), jnp.float32, low / len(pieces), top_value / len(pieces))
        return jnp.repeat(jnp.exp(heights), dims[dim] // shards_of).reshape((-1,) + (1,) * (len(dims) - dim - 1))

    gain = one(*pieces[0])
    for cut in pieces[1:]:
        gain = gain * one(*cut)
    return gain


def noise(key, dims, deviation, reach, cuts=(), kind=jnp.bfloat16):
    array = deviation * jax.random.normal(key, dims, jnp.float32)
    if cuts:
        array = array * steps_of(key, dims, cuts, -0.22, 0.18)
    return jnp.clip(array, -reach, reach).astype(kind)


def setup_inputs(seed: int = 0, part: int = 0) -> dict:
    key_of = jax.random.split(jax.random.key(seed), 6)
    part_splits = jax.random.split(jax.random.fold_in(key_of[5], part), 6)
    return {
        "queries": draw_queries(jax.random.fold_in(jax.random.fold_in(key_of[5], part), 71), part),
        "keys": draw_keys(jax.random.fold_in(jax.random.fold_in(key_of[5], part), 71), part),
        "values": noise(part_splits[2], (NKB, BLOCK, D), 1.0, 6.0, ((0, 32), (1, 8))),
        "mask_cols": draw_mask_cols(jax.random.fold_in(key_of[5], 71), part),
        "mask_counts": draw_mask_counts(jax.random.fold_in(key_of[5], 71), part),
    }


def reference(queries, keys, values, mask_cols, mask_counts):
    heads = D // DH
    scale = 1.0 / (DH ** 0.5)
    total_keys = keys.shape[0]
    query_float = queries.reshape(QB * BLOCK, heads, DH).astype(jnp.float32)
    listed = jnp.arange(LIST)[None, :] < mask_counts[:, None]
    hits = (mask_cols[:, :, None] == jnp.arange(total_keys, dtype=jnp.int32)[None, None, :]) & listed[:, :, None]
    allowed = jnp.any(hits, axis=1)
    groups = total_keys // KB_DEV
    key_groups = keys.reshape(groups, KB_DEV * BLOCK, heads, DH)
    value_groups = values.reshape(groups, KB_DEV * BLOCK, heads, DH)
    allow_groups = allowed.reshape(QB, groups, KB_DEV).transpose(1, 0, 2)

    def step(carry, item):
        top, norm, summed = carry
        key_block, value_block, allow_block = item
        key_open = jnp.repeat(allow_block, BLOCK, axis=1)
        live = jnp.repeat(key_open, BLOCK, axis=0)[None]
        scores = jnp.einsum("qhd,khd->hqk", query_float, key_block.astype(jnp.float32)) * scale
        scores = jnp.where(live, scores, -1e30)
        group_top = jnp.max(scores, axis=-1)
        weights = jnp.where(live, jnp.exp(scores - group_top[..., None]), 0.0)
        group_total = jnp.sum(weights, axis=-1)
        rounded = lax.optimization_barrier(weights.astype(jnp.bfloat16))
        partial_sum = jnp.einsum("hqk,khd->qhd", rounded.astype(jnp.float32), value_block.astype(jnp.float32))
        safe = jnp.maximum(group_total.T, 1.0)
        group_out = lax.optimization_barrier((partial_sum / safe[..., None]).astype(jnp.bfloat16)).astype(jnp.float32)
        group_lse = group_top.T + jnp.log(safe)
        newtop = jnp.maximum(top, group_lse)
        old_weight = jnp.exp(top - newtop)
        new_weight = jnp.exp(group_lse - newtop)
        norm = norm * old_weight + new_weight
        summed = summed * old_weight[..., None] + group_out * new_weight[..., None]
        return (newtop, norm, summed), None

    start = (jnp.full((QB * BLOCK, heads), -1e30, jnp.float32), jnp.zeros((QB * BLOCK, heads), jnp.float32), jnp.zeros((QB * BLOCK, heads, DH), jnp.float32))
    (top, norm, summed), _ = lax.scan(step, start, (key_groups, value_groups, allow_groups))
    return (summed / norm[..., None]).reshape(QB, BLOCK, D).astype(jnp.bfloat16)
```

```python
import functools

import jax
import jax.numpy as jnp
from jax import lax
from jax.experimental import pallas as pl
from jax.experimental.pallas import tpu as pltpu
from jax.sharding import Mesh
from jax.sharding import PartitionSpec as P

DH = 128
LOG2E = 1.4426950408889634
CLOSED = -1e30
VMEM_LIMIT = 48 * 1024 * 1024


def pack_kernel(q_ref, k_ref, v_ref, out_ref):
    n_head, _, width = out_ref.shape
    blocks, tokens, _ = k_ref.shape
    qb, qt, _ = q_ref.shape
    queries = jnp.concatenate([q_ref[i].astype(jnp.float32) for i in range(qb)], axis=0)
    queries = queries.astype(jnp.bfloat16)
    for z in range(n_head):
        columns = pl.ds(z * width, width)
        for b in range(blocks):
            out_ref[z, pl.ds(b * tokens, tokens), :] = k_ref[b, :, columns]
            out_ref[z, pl.ds((blocks + b) * tokens, tokens), :] = v_ref[b, :, columns]
        out_ref[z, pl.ds(2 * blocks * tokens, qb * qt), :] = queries[:, z * width : (z + 1) * width]


def attend_kernel(kv_rows, q_ref, kv_ref, bias_ref, out_ref):
    n_x, n_z = kv_ref.shape[0], kv_ref.shape[1]
    rows, width = q_ref.shape
    heads = width // DH
    keys = n_z * kv_rows
    period = bias_ref.shape[0]
    scale = LOG2E / DH**0.5
    lane = lax.broadcasted_iota(jnp.int32, (rows, DH), 1)
    stats = jnp.zeros((rows, DH), jnp.float32)
    for h in range(heads):
        columns = pl.ds(h * DH, DH)
        query = q_ref[:, columns]
        scores = []
        for x in range(n_x):
            key = kv_ref[x, :, pl.ds(0, kv_rows), columns].reshape(keys, DH)
            s = lax.dot_general(query, key, (((1,), (1,)), ((), ())), preferred_element_type=jnp.float32)
            s = s.reshape(rows // period, period, keys) + bias_ref[:, x][None]
            scores.append(s.reshape(rows, keys))
        top = functools.reduce(jnp.maximum, scores)
        top = jnp.max(top, axis=1, keepdims=True)
        total = jnp.zeros((rows, 1), jnp.float32)
        partial = jnp.zeros((rows, DH), jnp.float32)
        for x in range(n_x):
            value = kv_ref[x, :, pl.ds(kv_rows, kv_rows), columns].reshape(keys, DH)
            weight = jnp.exp2((scores[x] - top) * scale)
            total = total + jnp.sum(weight, axis=1, keepdims=True)
            partial = partial + jnp.dot(
                weight.astype(jnp.bfloat16), value, preferred_element_type=jnp.float32
            )
        out_ref[:, columns] = (partial / total).astype(jnp.bfloat16)
        lse = top * (1.0 / DH**0.5) + jnp.log(total)
        high = lse.astype(jnp.bfloat16).astype(jnp.float32)
        rest = lse - high
        middle = rest.astype(jnp.bfloat16).astype(jnp.float32)
        low = rest - middle
        for part, value in enumerate((high, middle, low)):
            stats = jnp.where(lane == h + part * heads, value, stats)
    out_ref[:, pl.ds(width, DH)] = stats.astype(jnp.bfloat16)


def merge_kernel(n_y, heads, part_ref, out_ref):
    n_z = part_ref.shape[0] // n_y
    width = heads * DH
    qb, qt, _ = out_ref.shape
    for z in range(n_z):
        lse = []
        for y in range(n_y):
            stats = part_ref[y * n_z + z, :, pl.ds(width, DH)].astype(jnp.float32)
            lse.append(
                stats[:, :heads] + stats[:, heads : 2 * heads] + stats[:, 2 * heads : 3 * heads]
            )
        top = functools.reduce(jnp.maximum, lse)
        weight = [jnp.exp(item - top) for item in lse]
        norm = functools.reduce(jnp.add, weight)
        for h in range(heads):
            summed = jnp.zeros((qb * qt, DH), jnp.float32)
            for y in range(n_y):
                out = part_ref[y * n_z + z, :, pl.ds(h * DH, DH)].astype(jnp.float32)
                summed = summed + out * weight[y][:, h : h + 1]
            done = summed / norm[:, h : h + 1]
            for i in range(qb):
                out_ref[i, :, pl.ds(z * width + h * DH, DH)] = done[i * qt : (i + 1) * qt].astype(
                    jnp.bfloat16
                )


def call(kernel, out_shape, *args, flops=0):
    vmem = pl.BlockSpec(memory_space=pltpu.VMEM)
    size = sum(a.size * a.dtype.itemsize for a in args)
    size += sum(o.size * o.dtype.itemsize for o in jax.tree.leaves(out_shape))
    return pl.pallas_call(
        kernel,
        out_shape=out_shape,
        in_specs=[vmem] * len(args),
        out_specs=jax.tree.map(lambda _: vmem, out_shape),
        compiler_params=pltpu.CompilerParams(vmem_limit_bytes=VMEM_LIMIT),
        cost_estimate=pl.CostEstimate(flops=flops, bytes_accessed=size, transcendentals=0),
    )(*args)


def local(queries, keys, values, mask_cols, mask_counts):
    n_z, n_x, n_y = lax.axis_size("head"), lax.axis_size("x"), lax.axis_size("y")
    qb, qt, d = queries.shape
    blocks, tokens, _ = keys.shape
    width = d // n_z
    heads = width // DH
    kv_rows = blocks * tokens
    own_rows = qb * qt
    struct = functools.partial(jax.ShapeDtypeStruct, dtype=jnp.bfloat16)

    packed = call(pack_kernel, struct((n_z, 2 * kv_rows + own_rows, width)), queries, keys, values)
    sorted_ = lax.all_to_all(packed, "head", 0, 0)
    query = sorted_[:, 2 * kv_rows :].reshape(n_z * own_rows, width)
    kv = sorted_[:, : 2 * kv_rows]
    query_all = lax.all_to_all(
        jnp.broadcast_to(query[None], (n_y,) + query.shape), "y", 0, 0
    )
    kv_all = lax.all_gather(kv, "x")

    owned = (jnp.arange(n_x)[:, None] * n_y + lax.axis_index("y")) * blocks + jnp.arange(blocks)
    listed = jnp.arange(mask_cols.shape[1])[None, :] < mask_counts[:, None]
    hit = (mask_cols[:, :, None, None] == owned[None, None]) & listed[:, :, None, None]
    allowed = jnp.any(hit, axis=1)
    bias = jnp.where(allowed, 0.0, CLOSED).astype(jnp.float32)
    bias = jnp.broadcast_to(
        bias[:, None, :, None, :, None], (n_z * qb, qt, n_x, n_z, blocks, tokens)
    ).reshape(n_z * own_rows, n_x, n_z * kv_rows)

    rows = n_y * n_z * own_rows
    part = call(
        functools.partial(attend_kernel, kv_rows),
        struct((rows, width + DH)),
        query_all.reshape(rows, width),
        kv_all,
        bias,
        flops=4 * rows * n_x * n_z * kv_rows * width,
    )
    part = lax.all_to_all(
        part.reshape(n_y * n_z, own_rows, width + DH), ("y", "head"), 0, 0
    )
    return call(functools.partial(merge_kernel, n_y, heads), struct((qb, qt, d)), part)


def solution(mesh):
    cfg, head, kv = (mesh.shape[name] for name in ("cfg", "head", "kv"))
    n_x = 4
    fine = Mesh(mesh.devices.reshape(cfg, head, n_x, kv // n_x), ("cfg", "head", "x", "y"))
    token = P(("cfg", "head"), ("x", "y"), None)
    block = P(("cfg", "x", "y"), "head", None)
    return jax.shard_map(
        local,
        mesh=fine,
        in_specs=(token, block, block, P(), P()),
        out_specs=token,
        check_vma=False,
    )
```

```python
import functools

import jax
import jax.numpy as jnp
from jax import lax
from jax.experimental import pallas as pl
from jax.experimental.pallas import tpu as pltpu
from jax.sharding import Mesh
from jax.sharding import PartitionSpec as P

DH = 128
LOG2E = 1.4426950408889634
CLOSED = -1e30
VMEM_LIMIT = 40 * 1024 * 1024
STAT_ROWS = 16
BF = jnp.bfloat16
F32 = jnp.float32


def pack_kernel(q_hbm, k_hbm, v_hbm, out_ref, q_ref, k_ref, v_ref, sems):
    copies = [
        pltpu.make_async_copy(k_hbm, k_ref, sems.at[0]),
        pltpu.make_async_copy(v_hbm, v_ref, sems.at[1]),
        pltpu.make_async_copy(q_hbm, q_ref, sems.at[2]),
    ]
    for copy in copies:
        copy.start()
    n_z, heads = out_ref.shape[:2]
    blocks, tokens, _ = k_ref.shape
    qb, qt, _ = q_ref.shape
    for part, ref in enumerate((k_ref, v_ref)):
        copies[part].wait()
        for z in range(n_z):
            for h in range(heads):
                columns = pl.ds((z * heads + h) * DH, DH)
                for b in range(blocks):
                    rows = pl.ds((part * blocks + b) * tokens, tokens)
                    out_ref[z, h, rows, :] = ref[b, :, columns]
    copies[2].wait()
    queries = jnp.concatenate([q_ref[i].astype(F32) for i in range(qb)], axis=0).astype(BF)
    for z in range(n_z):
        for h in range(heads):
            first = (z * heads + h) * DH
            out_ref[z, h, pl.ds(2 * blocks * tokens, qb * qt), :] = queries[:, first : first + DH]


def unpack_kernel(kv_rows, sorted_ref, k_ref, v_ref, q_ref):
    n_z, heads, rows, _ = sorted_ref.shape
    own = rows - 2 * kv_rows
    for h in range(heads):
        for z in range(n_z):
            k_ref[h, pl.ds(z * kv_rows, kv_rows), :] = sorted_ref[z, h, pl.ds(0, kv_rows), :]
            v_ref[h, pl.ds(z * kv_rows, kv_rows), :] = sorted_ref[z, h, pl.ds(kv_rows, kv_rows), :]
        query = jnp.concatenate(
            [sorted_ref[z, h, pl.ds(2 * kv_rows, own), :].astype(F32) for z in range(n_z)], axis=0
        ).astype(BF)
        for y in range(q_ref.shape[0]):
            q_ref[y, h] = query


def attend_kernel(kv_rows, tokens, base, pieces, first, last, *refs):
    refs = list(refs)
    q_ref, bias_ref = refs[:2]
    kv = [refs[2 + 2 * i : 4 + 2 * i] for i in range(pieces)]
    rest = refs[2 + 2 * pieces :]
    if not first:
        top_in, total_in, acc_in = rest[:3]
        rest = rest[3:]
    n_to, heads, period, _ = q_ref.shape
    rows, keys = n_to * period, kv[0][0].shape[1]
    scale = LOG2E / DH**0.5
    lane = lax.broadcasted_iota(jnp.int32, (rows, DH), 1)
    blocks = kv_rows // tokens
    block = lax.broadcasted_iota(jnp.int32, (period, keys), 1) // tokens % blocks
    bias = []
    for i in range(pieces):
        place = (base + i) * blocks
        item = jnp.broadcast_to(bias_ref[:, place : place + 1], (period, keys))
        for b in range(1, blocks):
            item = jnp.where(block == b, bias_ref[:, place + b : place + b + 1], item)
        bias.append(item)
    tops = jnp.zeros((rows, DH), F32)
    totals = jnp.ones((rows, DH), F32)
    for h in range(heads):
        query = q_ref[:, h].reshape(rows, DH)
        scores = []
        for i in range(pieces):
            s = lax.dot_general(
                query, kv[i][0][h], (((1,), (1,)), ((), ())), preferred_element_type=F32
            )
            s = s.reshape(n_to, period, keys) + bias[i][None]
            scores.append(s.reshape(rows, keys))
        top = jnp.max(functools.reduce(jnp.maximum, scores), axis=1, keepdims=True)
        sums = jnp.zeros((rows, keys), F32)
        partial = jnp.zeros((rows, DH), F32)
        if not first:
            before = top_in[:, h : h + 1]
            top = jnp.maximum(top, before)
            fade = jnp.exp2((before - top) * scale)
            partial = acc_in[h] * fade
        for i in range(pieces):
            weight = jnp.exp2((scores[i] - top) * scale)
            sums = sums + weight
            partial = partial + jnp.dot(weight.astype(BF), kv[i][1][h], preferred_element_type=F32)
        total = jnp.sum(sums, axis=1, keepdims=True)
        if not first:
            total = total + total_in[:, h : h + 1] * fade
        tops = jnp.where(lane == h, top, tops)
        totals = jnp.where(lane == h, total, totals)
        if not last:
            rest[2][h] = partial
            continue
        out = (partial / total).astype(BF)
        for to in range(n_to):
            rest[0][to, pl.ds(h * period, period), :] = out[to * period : (to + 1) * period]
    if not last:
        rest[0][...] = tops
        rest[1][...] = totals
        return
    out_ref = rest[0]
    lse = tops * (1.0 / DH**0.5) + jnp.log(totals)
    high = lse.astype(BF).astype(F32)
    rest = lse - high
    middle = rest.astype(BF).astype(F32)
    stats = high + pltpu.roll(middle, heads, 1) + pltpu.roll(rest - middle, 2 * heads, 1)
    turned = stats.T[:STAT_ROWS]
    per = DH // period
    for to in range(n_to):
        item = turned[:, to // per * DH : (to // per + 1) * DH]
        if to % per:
            item = pltpu.roll(item, DH - to % per * period, 1)
        out_ref[to, pl.ds(heads * period, STAT_ROWS), :] = item.astype(BF)


def merge_kernel(heads, part_ref, out_ref):
    n_from = part_ref.shape[0]
    n_z, own, _ = out_ref.shape
    rows = n_z * own
    stats = jnp.concatenate(
        [part_ref[y, pl.ds(heads * rows, STAT_ROWS), :].astype(F32) for y in range(n_from)], axis=0
    ).T[:rows]
    lse = stats + pltpu.roll(stats, DH - heads, 1) + pltpu.roll(stats, DH - 2 * heads, 1)
    top = lse
    for step in (STAT_ROWS, 2 * STAT_ROWS, 4 * STAT_ROWS):
        top = jnp.maximum(top, pltpu.roll(top, step, 1))
    weight = jnp.exp(lse - top)
    norm = weight
    for step in (STAT_ROWS, 2 * STAT_ROWS, 4 * STAT_ROWS):
        norm = norm + pltpu.roll(norm, step, 1)
    weight = weight / norm
    for h in range(heads):
        summed = jnp.zeros((rows, DH), F32)
        for y in range(n_from):
            place = y * STAT_ROWS + h
            out = part_ref[y, pl.ds(h * rows, rows), :].astype(F32)
            summed = summed + out * weight[:, place : place + 1]
        done = summed.astype(BF)
        for z in range(n_z):
            out_ref[z, :, pl.ds(h * DH, DH)] = done[z * own : (z + 1) * own]


def finish_kernel(in_ref, out_ref):
    n_z, _, width = in_ref.shape
    qb, qt, _ = out_ref.shape
    for z in range(n_z):
        rows = in_ref[z].astype(F32)
        for i in range(qb):
            out_ref[i, :, pl.ds(z * width, width)] = rows[i * qt : (i + 1) * qt].astype(BF)


def call(kernel, out_shape, *args, flops=0, scratch=(), space=pltpu.VMEM, vmem=VMEM_LIMIT):
    whole = pl.BlockSpec(memory_space=pltpu.VMEM)
    size = sum(a.size * a.dtype.itemsize for a in args)
    size += sum(o.size * o.dtype.itemsize for o in jax.tree.leaves(out_shape))
    return pl.pallas_call(
        kernel,
        out_shape=out_shape,
        in_specs=[pl.BlockSpec(memory_space=space)] * len(args),
        out_specs=jax.tree.map(lambda _: whole, out_shape),
        scratch_shapes=list(scratch),
        compiler_params=pltpu.CompilerParams(vmem_limit_bytes=vmem),
        cost_estimate=pl.CostEstimate(flops=flops, bytes_accessed=size, transcendentals=0),
    )(*args)


def shift(block, axis, by):
    count = lax.axis_size(axis)
    return lax.ppermute(block, axis, [(i, (i + by) % count) for i in range(count)])


def local(queries, keys, values, mask_cols, mask_counts):
    n_z, n_x, n_y = lax.axis_size("head"), lax.axis_size("x"), lax.axis_size("y")
    qb, qt, d = queries.shape
    blocks, tokens, _ = keys.shape
    heads = d // n_z // DH
    kv_rows = blocks * tokens
    own = qb * qt
    period = n_z * own
    rows = n_y * period
    n_keys = n_z * kv_rows
    struct = jax.ShapeDtypeStruct

    packed = call(
        pack_kernel,
        struct((n_z, heads, 2 * kv_rows + own, DH), BF),
        queries,
        keys,
        values,
        scratch=[
            pltpu.VMEM(queries.shape, BF),
            pltpu.VMEM(keys.shape, BF),
            pltpu.VMEM(values.shape, BF),
            pltpu.SemaphoreType.DMA((3,)),
        ],
        space=pltpu.HBM, vmem=62 * 1024 * 1024,
    )
    sorted_ = lax.all_to_all(packed, "head", 0, 0)
    key, value, query = call(
        functools.partial(unpack_kernel, kv_rows),
        (
            struct((heads, n_keys, DH), BF),
            struct((heads, n_keys, DH), BF),
            struct((n_y, heads, period, DH), BF),
        ),
        sorted_,
    )

    key_left = shift(key, "x", 1)
    value_right = shift(value, "x", -1)
    query_all = lax.all_to_all(query, "y", 0, 0)
    key_right = shift(key, "x", -1)
    value_left = shift(value, "x", 1)
    key_far = shift(key_left, "x", 1)
    value_far = shift(value_right, "x", -1)

    x = lax.axis_index("x")
    places = jnp.stack([x, (x + n_x - 1) % n_x, (x + 1) % n_x, (x + 2) % n_x])
    owned = (places[:, None] * n_y + lax.axis_index("y")) * blocks + jnp.arange(blocks)
    owned = owned.reshape(-1)
    listed = jnp.arange(mask_cols.shape[1])[None, :] < mask_counts[:, None]
    hit = (mask_cols[:, :, None] == owned) & listed[:, :, None]
    bias = jnp.where(jnp.any(hit, axis=1), 0.0, CLOSED).astype(F32)
    bias = jnp.repeat(bias, qt, axis=0)

    flops = 4 * rows * n_keys * heads * DH
    part = call(
        functools.partial(attend_kernel, kv_rows, tokens, 0, 4, True, True),
        struct((n_y, heads * period + STAT_ROWS, DH), BF),
        query_all,
        bias,
        key,
        value,
        key_left,
        value_left,
        key_right,
        value_right,
        key_far,
        value_far,
        flops=4 * flops,
    )
    part = lax.all_to_all(part, "y", 0, 0)
    merged = call(
        functools.partial(merge_kernel, heads), struct((n_z, own, heads * DH), BF), part
    )
    merged = lax.all_to_all(merged, "head", 0, 0)
    return call(finish_kernel, struct((qb, qt, d), BF), merged)


def solution(mesh):
    cfg, head, kv = (mesh.shape[name] for name in ("cfg", "head", "kv"))
    n_x = 4
    fine = Mesh(mesh.devices.reshape(cfg, head, n_x, kv // n_x), ("cfg", "head", "x", "y"))
    token = P(("cfg", "head"), ("x", "y"), None)
    block = P(("cfg", "x", "y"), "head", None)
    return jax.shard_map(
        local,
        mesh=fine,
        in_specs=(token, block, block, P(), P()),
        out_specs=token,
        check_vma=False,
    )
```

```python
import functools

import jax
import jax.numpy as jnp
from jax import lax
from jax.experimental import pallas as pl
from jax.experimental.pallas import tpu as pltpu
from jax.sharding import Mesh
from jax.sharding import PartitionSpec as P

DH = 128
SCALE = 1.4426950408889634 / DH**0.5
CLOSED = -1e30
VMEM_LIMIT = 20 * 1024 * 1024
STAT_ROWS = 16
BF = jnp.bfloat16
F32 = jnp.float32


def pack_kernel(q_hbm, k_hbm, v_hbm, out_ref, q_ref, k_ref, v_ref, sems):
    copies = [
        pltpu.make_async_copy(k_hbm, k_ref, sems.at[0]),
        pltpu.make_async_copy(v_hbm, v_ref, sems.at[1]),
        pltpu.make_async_copy(q_hbm, q_ref, sems.at[2]),
    ]
    for copy in copies:
        copy.start()
    n_z, heads = out_ref.shape[:2]
    blocks, tokens, _ = k_ref.shape
    qb, qt, _ = q_ref.shape
    for part, ref in enumerate((k_ref, v_ref)):
        copies[part].wait()
        for z in range(n_z):
            for h in range(heads):
                columns = pl.ds((z * heads + h) * DH, DH)
                for b in range(blocks):
                    rows = pl.ds((part * blocks + b) * tokens, tokens)
                    out_ref[z, h, rows, :] = ref[b, :, columns]
    copies[2].wait()
    queries = jnp.concatenate([q_ref[i].astype(F32) for i in range(qb)], axis=0).astype(BF)
    for z in range(n_z):
        for h in range(heads):
            first = (z * heads + h) * DH
            out_ref[z, h, pl.ds(2 * blocks * tokens, qb * qt), :] = queries[:, first : first + DH]


def unpack_kernel(kv_rows, sorted_ref, kv_ref):
    n_z, heads, _, _ = sorted_ref.shape
    for h in range(heads):
        for z in range(n_z):
            for part in range(2):
                rows = sorted_ref[z, h, pl.ds(part * kv_rows, kv_rows), :]
                kv_ref[part, h, pl.ds(z * kv_rows, kv_rows), :] = rows


def spread_kernel(kv_rows, sorted_ref, q_ref):
    n_z, heads, rows, _ = sorted_ref.shape
    for h in range(heads):
        query = jnp.concatenate(
            [sorted_ref[z, h, pl.ds(2 * kv_rows, rows - 2 * kv_rows), :].astype(F32) for z in range(n_z)],
            axis=0,
        ).astype(BF)
        for to in range(q_ref.shape[0]):
            q_ref[to, h] = query


def block_bias(bias_ref, piece, blocks, tokens, keys):
    place = piece * blocks
    block = lax.broadcasted_iota(jnp.int32, (bias_ref.shape[0], keys), 1) // tokens % blocks
    bias = jnp.broadcast_to(bias_ref[:, place : place + 1], block.shape)
    for b in range(1, blocks):
        bias = jnp.where(block == b, bias_ref[:, place + b : place + b + 1], bias)
    return bias


def scores_of(query, key, bias):
    s = lax.dot_general(query, key, (((1,), (1,)), ((), ())), preferred_element_type=F32)
    period, keys = bias.shape
    return (s.reshape(-1, period, keys) + bias[None]).reshape(s.shape)


def weigh(scores, top, value):
    weight = jnp.exp2((scores - top) * SCALE).astype(BF)
    ones = jnp.ones(value.shape, BF)
    return jnp.dot(weight, jnp.concatenate([value, ones], axis=1), preferred_element_type=F32)


def attend_kernel(blocks, tokens, q_ref, bias_ref, *refs):
    pieces, (top_ref, total_ref, sum_ref) = refs[:-3], refs[-3:]
    n_to, heads, period, _ = q_ref.shape
    rows, keys = n_to * period, pieces[0].shape[2]
    bias = [block_bias(bias_ref, i, blocks, tokens, keys) for i in range(len(pieces))]
    for h in range(heads):
        query = q_ref[:, h].reshape(rows, DH)
        scores = [scores_of(query, ref[0, h], item) for ref, item in zip(pieces, bias, strict=True)]
        top = jnp.max(functools.reduce(jnp.maximum, scores), axis=1, keepdims=True)
        both = jnp.zeros((rows, 2 * DH), F32)
        for s, ref in zip(scores, pieces, strict=True):
            both = both + weigh(s, top, ref[1, h])
        top_ref[h] = jnp.broadcast_to(top, (rows, DH))
        sum_ref[h] = both[:, :DH]
        total_ref[h] = both[:, DH:]


def last_kernel(blocks, tokens, piece, q_ref, bias_ref, key_ref, value_ref, top_ref, total_ref, sum_ref, out_ref):
    n_to, heads, period, _ = q_ref.shape
    rows, keys = n_to * period, key_ref.shape[1]
    bias = block_bias(bias_ref, piece, blocks, tokens, keys)
    lane = lax.broadcasted_iota(jnp.int32, (rows, DH), 1)
    tops = jnp.zeros((rows, DH), F32)
    totals = jnp.ones((rows, DH), F32)
    own = out_ref.shape[1] // (heads + 1)

    def put(h, item):
        for i in range(rows // own):
            out_ref[i, pl.ds(h * own, own), :] = item[i * own : (i + 1) * own]

    for h in range(heads):
        scores = scores_of(q_ref[:, h].reshape(rows, DH), key_ref[h], bias)
        before = top_ref[h]
        top = jnp.maximum(jnp.max(scores, axis=1, keepdims=True), before)
        fade = jnp.exp2((before - top) * SCALE)
        both = weigh(scores, jnp.concatenate([top] * (keys // DH), axis=1), value_ref[h])
        total = total_ref[h] * fade + both[:, DH:]
        out = ((sum_ref[h] * fade + both[:, :DH]) / total).astype(BF)
        put(h, out)
        tops = jnp.where(lane == h, top, tops)
        totals = jnp.where(lane == h, total, totals)
    lse = tops * (1.0 / DH**0.5) + jnp.log(totals)
    high = lse.astype(BF).astype(F32)
    rest = lse - high
    middle = rest.astype(BF).astype(F32)
    stats = high + pltpu.roll(middle, heads, 1) + pltpu.roll(rest - middle, 2 * heads, 1)
    put(heads, stats.astype(BF))


def merge_kernel(n_from, part_ref, out_ref):
    n_z, heads = part_ref.shape[0] // n_from, part_ref.shape[1] // (out_ref.shape[0] * out_ref.shape[1]) - 1
    qb, qt, _ = out_ref.shape
    own = qb * qt
    for z in range(n_z):
        lse = []
        for y in range(n_from):
            stats = part_ref[y * n_z + z, pl.ds(heads * own, own), :].astype(F32)
            lse.append(stats + pltpu.roll(stats, DH - heads, 1) + pltpu.roll(stats, DH - 2 * heads, 1))
        top = functools.reduce(jnp.maximum, lse)
        weight = [jnp.exp(item - top) for item in lse]
        norm = functools.reduce(jnp.add, weight)
        weight = [item / norm for item in weight]
        for h in range(heads):
            summed = jnp.zeros((own, DH), F32)
            for y in range(n_from):
                out = part_ref[y * n_z + z, pl.ds(h * own, own), :].astype(F32)
                summed = summed + out * weight[y][:, h : h + 1]
            for i in range(qb):
                place = pl.ds((z * heads + h) * DH, DH)
                out_ref[i, :, place] = summed[i * qt : (i + 1) * qt].astype(BF)


def call(kernel, out_shape, *args, flops=0, scratch=(), space=pltpu.VMEM, vmem=VMEM_LIMIT):
    whole = pl.BlockSpec(memory_space=pltpu.VMEM)
    size = sum(a.size * a.dtype.itemsize for a in args)
    size += sum(o.size * o.dtype.itemsize for o in jax.tree.leaves(out_shape))
    return pl.pallas_call(
        kernel,
        out_shape=out_shape,
        in_specs=[pl.BlockSpec(memory_space=space)] * len(args),
        out_specs=jax.tree.map(lambda _: whole, out_shape),
        scratch_shapes=list(scratch),
        compiler_params=pltpu.CompilerParams(vmem_limit_bytes=vmem),
        cost_estimate=pl.CostEstimate(flops=flops, bytes_accessed=size, transcendentals=0),
    )(*args)


def shift(block, axis, by):
    count = lax.axis_size(axis)
    return lax.ppermute(block, axis, [(i, (i + by) % count) for i in range(count)])


def local(queries, keys, values, mask_cols, mask_counts):
    n_z, n_x, n_y = lax.axis_size("head"), lax.axis_size("x"), lax.axis_size("y")
    qb, qt, d = queries.shape
    blocks, tokens, _ = keys.shape
    heads = d // n_z // DH
    kv_rows = blocks * tokens
    own = qb * qt
    period = n_z * own
    rows = n_y * period
    n_keys = n_z * kv_rows
    struct = jax.ShapeDtypeStruct

    packed = call(
        pack_kernel,
        struct((n_z, heads, 2 * kv_rows + own, DH), BF),
        queries,
        keys,
        values,
        scratch=[
            pltpu.VMEM(queries.shape, BF),
            pltpu.VMEM(keys.shape, BF),
            pltpu.VMEM(values.shape, BF),
            pltpu.SemaphoreType.DMA((3,)),
        ],
        space=pltpu.HBM, vmem=62 * 1024 * 1024,
    )
    sorted_ = lax.all_to_all(packed, "head", 0, 0)
    kv = call(
        functools.partial(unpack_kernel, kv_rows), struct((2, heads, n_keys, DH), BF), sorted_
    )
    query = call(
        functools.partial(spread_kernel, kv_rows), struct((n_y, heads, period, DH), BF), sorted_
    )

    pair_left = shift(kv, "x", 1)
    pair_right = shift(kv, "x", -1)
    query_all = lax.all_to_all(query, "y", 0, 0)
    key_far = shift(pair_left[0], "x", 1)
    value_far = shift(pair_right[1], "x", -1)

    x = lax.axis_index("x")
    places = jnp.stack([x, (x + n_x - 1) % n_x, (x + 1) % n_x, (x + 2) % n_x])
    owned = (places[:, None] * n_y + lax.axis_index("y")) * blocks + jnp.arange(blocks)
    owned = owned.reshape(-1)
    listed = jnp.arange(mask_cols.shape[1])[None, :] < mask_counts[:, None]
    hit = (mask_cols[:, :, None] == owned) & listed[:, :, None]
    bias = jnp.where(jnp.any(hit, axis=1), 0.0, CLOSED).astype(F32)
    bias = jnp.repeat(bias, qt, axis=0)

    flops = 4 * rows * n_keys * heads * DH
    state = call(
        functools.partial(attend_kernel, blocks, tokens),
        (struct((heads, rows, DH), F32),) * 3,
        query_all,
        bias,
        kv,
        pair_left,
        pair_right,
        flops=3 * flops,
    )
    part = call(
        functools.partial(last_kernel, blocks, tokens, 3),
        struct((n_y * n_z, (heads + 1) * own, DH), BF),
        query_all,
        bias,
        key_far,
        value_far,
        *state,
        flops=flops,
    )
    part = lax.all_to_all(part, ("y", "head"), 0, 0)
    return call(functools.partial(merge_kernel, n_y), struct((qb, qt, d), BF), part)


def solution(mesh):
    cfg, head, kv = (mesh.shape[name] for name in ("cfg", "head", "kv"))
    n_x = 4
    fine = Mesh(mesh.devices.reshape(cfg, head, n_x, kv // n_x), ("cfg", "head", "x", "y"))
    token = P(("cfg", "head"), ("x", "y"), None)
    block = P(("cfg", "x", "y"), "head", None)
    return jax.shard_map(
        local,
        mesh=fine,
        in_specs=(token, block, block, P(), P()),
        out_specs=token,
        check_vma=False,
    )
```

```python
import functools

import jax
import jax.numpy as jnp
from jax import lax
from jax.experimental import pallas as pl
from jax.experimental.pallas import tpu as pltpu
from jax.sharding import Mesh
from jax.sharding import PartitionSpec as P

DH = 128
SCALE = 1.4426950408889634 / DH**0.5
CLOSED = -1e30
VMEM_LIMIT = 20 * 1024 * 1024
STAT_ROWS = 16
BF = jnp.bfloat16
F32 = jnp.float32


def pack_kernel(q_hbm, k_hbm, v_hbm, out_ref, q_ref, k_ref, v_ref, sems):
    copies = [
        pltpu.make_async_copy(k_hbm, k_ref, sems.at[0]),
        pltpu.make_async_copy(v_hbm, v_ref, sems.at[1]),
        pltpu.make_async_copy(q_hbm, q_ref, sems.at[2]),
    ]
    for copy in copies:
        copy.start()
    n_z, heads = out_ref.shape[:2]
    blocks, tokens, _ = k_ref.shape
    qb, qt, _ = q_ref.shape
    for part, ref in enumerate((k_ref, v_ref)):
        copies[part].wait()
        for z in range(n_z):
            for h in range(heads):
                columns = pl.ds((z * heads + h) * DH, DH)
                for b in range(blocks):
                    rows = pl.ds((part * blocks + b) * tokens, tokens)
                    out_ref[z, h, rows, :] = ref[b, :, columns]
    copies[2].wait()
    queries = jnp.concatenate([q_ref[i].astype(F32) for i in range(qb)], axis=0).astype(BF)
    for z in range(n_z):
        for h in range(heads):
            first = (z * heads + h) * DH
            out_ref[z, h, pl.ds(2 * blocks * tokens, qb * qt), :] = queries[:, first : first + DH]


def unpack_kernel(kv_rows, sorted_ref, kv_ref):
    n_z, heads, _, _ = sorted_ref.shape
    for h in range(heads):
        for z in range(n_z):
            for part in range(2):
                rows = sorted_ref[z, h, pl.ds(part * kv_rows, kv_rows), :]
                kv_ref[h, part, pl.ds(z * kv_rows, kv_rows), :] = rows


def spread_kernel(kv_rows, sorted_ref, q_ref):
    n_z, heads, rows, _ = sorted_ref.shape
    for h in range(heads):
        query = jnp.concatenate(
            [sorted_ref[z, h, pl.ds(2 * kv_rows, rows - 2 * kv_rows), :].astype(F32) for z in range(n_z)],
            axis=0,
        ).astype(BF)
        for to in range(q_ref.shape[0]):
            q_ref[to, h] = query


def take_kernel(first, pair_ref, out_ref):
    out_ref[...] = pair_ref[pl.ds(first, out_ref.shape[0])]


def block_bias(bias_ref, piece, blocks, tokens, keys):
    place = piece * blocks
    block = lax.broadcasted_iota(jnp.int32, (bias_ref.shape[0], keys), 1) // tokens % blocks
    bias = jnp.broadcast_to(bias_ref[:, place : place + 1], block.shape)
    for b in range(1, blocks):
        bias = jnp.where(block == b, bias_ref[:, place + b : place + b + 1], bias)
    return bias


def scores_of(query, key, bias):
    s = lax.dot_general(query, key, (((1,), (1,)), ((), ())), preferred_element_type=F32)
    period, keys = bias.shape
    return (s.reshape(-1, period, keys) + bias[None]).reshape(s.shape)


def weigh(scores, top, value):
    weight = jnp.exp2((scores - top) * SCALE).astype(BF)
    ones = jnp.ones(value.shape, BF)
    return jnp.dot(weight, jnp.concatenate([value, ones], axis=1), preferred_element_type=F32)


def attend_kernel(blocks, tokens, q_ref, bias_ref, *refs):
    pieces, (top_ref, total_ref, sum_ref) = refs[:-3], refs[-3:]
    n_to, heads, period, _ = q_ref.shape
    rows, keys = n_to * period, pieces[0].shape[2]
    bias = [block_bias(bias_ref, i, blocks, tokens, keys) for i in range(len(pieces))]
    for h in range(heads):
        query = q_ref[:, h].reshape(rows, DH)
        scores = [scores_of(query, ref[h, 0], item) for ref, item in zip(pieces, bias, strict=True)]
        top = jnp.max(functools.reduce(jnp.maximum, scores), axis=1, keepdims=True)
        both = jnp.zeros((rows, 2 * DH), F32)
        for s, ref in zip(scores, pieces, strict=True):
            both = both + weigh(s, top, ref[h, 1])
        top_ref[h] = jnp.broadcast_to(top, (rows, DH))
        sum_ref[h] = both[:, :DH]
        total_ref[h] = both[:, DH:]


def last_kernel(blocks, tokens, piece, q_ref, bias_ref, low_ref, high_ref, top_ref, total_ref, sum_ref, out_ref):
    n_to, heads, period, _ = q_ref.shape
    rows, keys = n_to * period, low_ref.shape[2]
    bias = block_bias(bias_ref, piece, blocks, tokens, keys)
    lane = lax.broadcasted_iota(jnp.int32, (rows, DH), 1)
    tops = jnp.zeros((rows, DH), F32)
    totals = jnp.ones((rows, DH), F32)
    own = out_ref.shape[1] // (heads + 1)

    def put(h, item):
        for i in range(rows // own):
            out_ref[i, pl.ds(h * own, own), :] = item[i * own : (i + 1) * own]

    for h in range(heads):
        cut = low_ref.shape[0]
        pair = low_ref.at[h] if h < cut else high_ref.at[h - cut]
        scores = scores_of(q_ref[:, h].reshape(rows, DH), pair[0], bias)
        before = top_ref[h]
        top = jnp.maximum(jnp.max(scores, axis=1, keepdims=True), before)
        fade = jnp.exp2((before - top) * SCALE)
        both = weigh(scores, jnp.concatenate([top] * (keys // DH), axis=1), pair[1])
        total = total_ref[h] * fade + both[:, DH:]
        out = ((sum_ref[h] * fade + both[:, :DH]) / total).astype(BF)
        put(h, out)
        tops = jnp.where(lane == h, top, tops)
        totals = jnp.where(lane == h, total, totals)
    lse = tops * (1.0 / DH**0.5) + jnp.log(totals)
    high = lse.astype(BF).astype(F32)
    rest = lse - high
    middle = rest.astype(BF).astype(F32)
    stats = high + pltpu.roll(middle, heads, 1) + pltpu.roll(rest - middle, 2 * heads, 1)
    put(heads, stats.astype(BF))


def merge_kernel(n_from, part_ref, out_ref):
    n_z = part_ref.shape[0] // n_from
    qb, qt, _ = out_ref.shape
    own = qb * qt
    heads = part_ref.shape[1] // own - 1

    def rows_of(item):
        rows = part_ref[:, pl.ds(item * own, own), :].astype(F32)
        return rows.reshape(n_from, n_z * own, DH)

    stats = rows_of(heads)
    lse = stats + pltpu.roll(stats, DH - heads, 2) + pltpu.roll(stats, DH - 2 * heads, 2)
    weight = jnp.exp(lse - jnp.max(lse, axis=0, keepdims=True))
    weight = weight / jnp.sum(weight, axis=0, keepdims=True)
    for h in range(heads):
        summed = jnp.sum(rows_of(h) * weight[:, :, h : h + 1], axis=0)
        for z in range(n_z):
            for i in range(qb):
                place = pl.ds((z * heads + h) * DH, DH)
                first = z * own + i * qt
                out_ref[i, :, place] = summed[first : first + qt].astype(BF)


def call(kernel, out_shape, *args, flops=0, light=False, scratch=(), space=pltpu.VMEM, vmem=VMEM_LIMIT):
    whole = pl.BlockSpec(memory_space=pltpu.VMEM)
    size = sum(a.size * a.dtype.itemsize for a in args)
    size += sum(o.size * o.dtype.itemsize for o in jax.tree.leaves(out_shape))
    if light:
        size = 0
    return pl.pallas_call(
        kernel,
        out_shape=out_shape,
        in_specs=[pl.BlockSpec(memory_space=space)] * len(args),
        out_specs=jax.tree.map(lambda _: whole, out_shape),
        scratch_shapes=list(scratch),
        compiler_params=pltpu.CompilerParams(vmem_limit_bytes=vmem),
        cost_estimate=pl.CostEstimate(flops=flops, bytes_accessed=size, transcendentals=0),
    )(*args)


def shift(block, axis, by):
    count = lax.axis_size(axis)
    return lax.ppermute(block, axis, [(i, (i + by) % count) for i in range(count)])


def local(queries, keys, values, mask_cols, mask_counts):
    n_z, n_x, n_y = lax.axis_size("head"), lax.axis_size("x"), lax.axis_size("y")
    qb, qt, d = queries.shape
    blocks, tokens, _ = keys.shape
    heads = d // n_z // DH
    kv_rows = blocks * tokens
    own = qb * qt
    period = n_z * own
    rows = n_y * period
    n_keys = n_z * kv_rows
    struct = jax.ShapeDtypeStruct

    packed = call(
        pack_kernel,
        struct((n_z, heads, 2 * kv_rows + own, DH), BF),
        queries,
        keys,
        values,
        scratch=[
            pltpu.VMEM(queries.shape, BF),
            pltpu.VMEM(keys.shape, BF),
            pltpu.VMEM(values.shape, BF),
            pltpu.SemaphoreType.DMA((3,)),
        ],
        space=pltpu.HBM, vmem=62 * 1024 * 1024,
    )
    sorted_ = lax.all_to_all(packed, "head", 0, 0)
    kv = call(
        functools.partial(unpack_kernel, kv_rows), struct((heads, 2, n_keys, DH), BF), sorted_
    )
    query = call(
        functools.partial(spread_kernel, kv_rows), struct((n_y, heads, period, DH), BF), sorted_
    )

    pair_left = shift(kv, "x", 1)
    pair_right = shift(kv, "x", -1)
    query_all = lax.all_to_all(query, "y", 0, 0)
    cut = (heads + 1) // 2
    far_low, far_high = (
        shift(
            call(
                functools.partial(take_kernel, first),
                struct((count,) + kv.shape[1:], BF),
                pair,
                flops=2 * 10**10,
            ),
            "x",
            by,
        )
        for pair, first, count, by in ((pair_left, 0, cut, 1), (pair_right, cut, heads - cut, -1))
    )

    x = lax.axis_index("x")
    places = jnp.stack([x, (x + n_x - 1) % n_x, (x + 1) % n_x, (x + 2) % n_x])
    owned = (places[:, None] * n_y + lax.axis_index("y")) * blocks + jnp.arange(blocks)
    owned = owned.reshape(-1)
    listed = jnp.arange(mask_cols.shape[1])[None, :] < mask_counts[:, None]
    hit = (mask_cols[:, :, None] == owned) & listed[:, :, None]
    bias = jnp.where(jnp.any(hit, axis=1), 0.0, CLOSED).astype(F32)
    bias = jnp.repeat(bias, qt, axis=0)

    flops = 4 * rows * n_keys * heads * DH
    state = call(
        functools.partial(attend_kernel, blocks, tokens),
        (struct((heads, rows, DH), F32),) * 3,
        query_all,
        bias,
        kv,
        pair_left,
        pair_right,
        light=True,
    )
    part = call(
        functools.partial(last_kernel, blocks, tokens, 3),
        struct((n_y * n_z, (heads + 1) * own, DH), BF),
        query_all,
        bias,
        far_low,
        far_high,
        *state,
        flops=flops,
    )
    part = lax.all_to_all(part, ("y", "head"), 0, 0)
    return call(functools.partial(merge_kernel, n_y), struct((qb, qt, d), BF), part)


def solution(mesh):
    cfg, head, kv = (mesh.shape[name] for name in ("cfg", "head", "kv"))
    n_x = 4
    fine = Mesh(mesh.devices.reshape(cfg, head, n_x, kv // n_x), ("cfg", "head", "x", "y"))
    token = P(("cfg", "head"), ("x", "y"), None)
    block = P(("cfg", "x", "y"), "head", None)
    return jax.shard_map(
        local,
        mesh=fine,
        in_specs=(token, block, block, P(), P()),
        out_specs=token,
        check_vma=False,
    )
```

```python
import functools

import jax
import jax.numpy as jnp
from jax import lax
from jax.experimental import pallas as pl
from jax.experimental.pallas import tpu as pltpu
from jax.sharding import Mesh
from jax.sharding import PartitionSpec as P

DH = 128
SCALE = 1.4426950408889634 / DH**0.5
CLOSED = -1e30
VMEM_LIMIT = 20 * 1024 * 1024
STAT_ROWS = 16
BF = jnp.bfloat16
F32 = jnp.float32


def pack_kernel(q_hbm, k_hbm, v_hbm, out_ref, q_ref, k_ref, v_ref, sems):
    copies = [
        pltpu.make_async_copy(k_hbm, k_ref, sems.at[0]),
        pltpu.make_async_copy(v_hbm, v_ref, sems.at[1]),
        pltpu.make_async_copy(q_hbm, q_ref, sems.at[2]),
    ]
    for copy in copies:
        copy.start()
    n_z, heads = out_ref.shape[:2]
    blocks, tokens, _ = k_ref.shape
    qb, qt, _ = q_ref.shape
    for part, ref in enumerate((k_ref, v_ref)):
        copies[part].wait()
        for z in range(n_z):
            for h in range(heads):
                columns = pl.ds((z * heads + h) * DH, DH)
                for b in range(blocks):
                    rows = pl.ds((part * blocks + b) * tokens, tokens)
                    out_ref[z, h, rows, :] = ref[b, :, columns]
    copies[2].wait()
    queries = jnp.concatenate([q_ref[i].astype(F32) for i in range(qb)], axis=0).astype(BF)
    for z in range(n_z):
        for h in range(heads):
            first = (z * heads + h) * DH
            out_ref[z, h, pl.ds(2 * blocks * tokens, qb * qt), :] = queries[:, first : first + DH]


def unpack_kernel(kv_rows, sorted_ref, kv_ref):
    n_z, heads, _, _ = sorted_ref.shape
    for h in range(heads):
        for z in range(n_z):
            for part in range(2):
                rows = sorted_ref[z, h, pl.ds(part * kv_rows, kv_rows), :]
                kv_ref[h, part, pl.ds(z * kv_rows, kv_rows), :] = rows


def spread_kernel(kv_rows, sorted_ref, q_ref):
    n_z, heads, rows, _ = sorted_ref.shape
    for h in range(heads):
        query = jnp.concatenate(
            [sorted_ref[z, h, pl.ds(2 * kv_rows, rows - 2 * kv_rows), :].astype(F32) for z in range(n_z)],
            axis=0,
        ).astype(BF)
        for to in range(q_ref.shape[0]):
            q_ref[to, h] = query


def take_kernel(first, pair_ref, out_ref):
    out_ref[...] = pair_ref[pl.ds(first, out_ref.shape[0])]


def block_bias(bias_ref, piece, blocks, tokens, keys):
    place = piece * blocks
    block = lax.broadcasted_iota(jnp.int32, (bias_ref.shape[0], keys), 1) // tokens % blocks
    bias = jnp.broadcast_to(bias_ref[:, place : place + 1], block.shape)
    for b in range(1, blocks):
        bias = jnp.where(block == b, bias_ref[:, place + b : place + b + 1], bias)
    return bias


def scores_of(query, key, bias):
    s = lax.dot_general(query, key, (((1,), (1,)), ((), ())), preferred_element_type=F32)
    period, keys = bias.shape
    return (s.reshape(-1, period, keys) + bias[None]).reshape(s.shape)


def weigh(scores, top, value):
    weight = jnp.exp2((scores - top) * SCALE).astype(BF)
    ones = jnp.ones(value.shape, BF)
    return jnp.dot(weight, jnp.concatenate([value, ones], axis=1), preferred_element_type=F32)


def attend_kernel(blocks, tokens, q_ref, bias_ref, *refs):
    pieces, (top_ref, total_ref, sum_ref) = refs[:-3], refs[-3:]
    n_to, heads, period, _ = q_ref.shape
    rows, keys = n_to * period, pieces[0].shape[2]
    bias = [block_bias(bias_ref, i, blocks, tokens, keys) for i in range(len(pieces))]
    for h in range(heads):
        query = q_ref[:, h].reshape(rows, DH)
        scores = [scores_of(query, ref[h, 0], item) for ref, item in zip(pieces, bias, strict=True)]
        top = jnp.max(functools.reduce(jnp.maximum, scores), axis=1, keepdims=True)
        both = jnp.zeros((rows, 2 * DH), F32)
        for s, ref in zip(scores, pieces, strict=True):
            both = both + weigh(s, top, ref[h, 1])
        top_ref[h] = jnp.broadcast_to(top, (rows, DH))
        sum_ref[h] = both[:, :DH]
        total_ref[h] = both[:, DH:]


def last_kernel(blocks, tokens, piece, q_ref, bias_ref, low_ref, high_ref, top_ref, total_ref, sum_ref, out_ref):
    n_to, heads, period, _ = q_ref.shape
    rows, keys = n_to * period, low_ref.shape[2]
    bias = block_bias(bias_ref, piece, blocks, tokens, keys)
    lane = lax.broadcasted_iota(jnp.int32, (rows, DH), 1)
    tops = jnp.zeros((rows, DH), F32)
    totals = jnp.ones((rows, DH), F32)
    n_dest, parts, qt, _ = out_ref.shape
    qb = parts // heads
    own = qb * qt
    for h in range(heads):
        cut = low_ref.shape[0]
        pair = low_ref.at[h] if h < cut else high_ref.at[h - cut]
        scores = scores_of(q_ref[:, h].reshape(rows, DH), pair[0], bias)
        before = top_ref[h]
        top = jnp.maximum(jnp.max(scores, axis=1, keepdims=True), before)
        fade = jnp.exp2((before - top) * SCALE)
        both = weigh(scores, jnp.concatenate([top] * (keys // DH), axis=1), pair[1])
        total = total_ref[h] * fade + both[:, DH:]
        out = (sum_ref[h] * fade + both[:, :DH]) / total
        out = out.reshape(n_dest, own, DH)
        for b in range(qb):
            out_ref[:, h * qb + b] = out[:, b * qt : (b + 1) * qt].astype(BF)
        tops = jnp.where(lane == h, top, tops)
        totals = jnp.where(lane == h, total, totals)
    lse = tops * (1.0 / DH**0.5) + jnp.log(totals)
    high = lse.astype(BF).astype(F32)
    rest = lse - high
    middle = rest.astype(BF).astype(F32)
    stats = high + pltpu.roll(middle, heads, 1) + pltpu.roll(rest - middle, 2 * heads, 1)
    stats = stats.reshape(n_dest, own, DH)
    joined = stats[:, :qt]
    for b in range(1, qb):
        joined = joined + pltpu.roll(stats, b * (DH // qb), 2)[:, b * qt : (b + 1) * qt]
    out_ref[:, heads * qb] = joined.astype(BF)


def merge_kernel(n_from, part_ref, out_ref):
    n_z = part_ref.shape[0] // n_from
    qb, qt, _ = out_ref.shape
    heads = part_ref.shape[1] // qb

    def rows_of(item):
        return part_ref[:, item].astype(F32).reshape(n_from, n_z, qt, DH)

    stats = rows_of(heads * qb)
    lse = stats + pltpu.roll(stats, DH - heads, 3) + pltpu.roll(stats, DH - 2 * heads, 3)
    weight = jnp.exp(lse - jnp.max(lse, axis=0, keepdims=True))
    weight = weight / jnp.sum(weight, axis=0, keepdims=True)
    for h in range(heads):
        for b in range(qb):
            lane = b * (DH // qb) + h
            summed = jnp.sum(rows_of(h * qb + b) * weight[..., lane : lane + 1], axis=0)
            for z in range(n_z):
                out_ref[b, :, pl.ds((z * heads + h) * DH, DH)] = summed[z].astype(BF)


def call(kernel, out_shape, *args, flops=0, light=False, scratch=(), space=pltpu.VMEM, vmem=VMEM_LIMIT):
    whole = pl.BlockSpec(memory_space=pltpu.VMEM)
    size = sum(a.size * a.dtype.itemsize for a in args)
    size += sum(o.size * o.dtype.itemsize for o in jax.tree.leaves(out_shape))
    if light:
        size = 0
    return pl.pallas_call(
        kernel,
        out_shape=out_shape,
        in_specs=[pl.BlockSpec(memory_space=space)] * len(args),
        out_specs=jax.tree.map(lambda _: whole, out_shape),
        scratch_shapes=list(scratch),
        compiler_params=pltpu.CompilerParams(vmem_limit_bytes=vmem),
        cost_estimate=pl.CostEstimate(flops=flops, bytes_accessed=size, transcendentals=0),
    )(*args)


def shift(block, axis, by):
    count = lax.axis_size(axis)
    return lax.ppermute(block, axis, [(i, (i + by) % count) for i in range(count)])


def local(queries, keys, values, mask_cols, mask_counts):
    n_z, n_x, n_y = lax.axis_size("head"), lax.axis_size("x"), lax.axis_size("y")
    qb, qt, d = queries.shape
    blocks, tokens, _ = keys.shape
    heads = d // n_z // DH
    kv_rows = blocks * tokens
    own = qb * qt
    period = n_z * own
    rows = n_y * period
    n_keys = n_z * kv_rows
    struct = jax.ShapeDtypeStruct

    packed = call(
        pack_kernel,
        struct((n_z, heads, 2 * kv_rows + own, DH), BF),
        queries,
        keys,
        values,
        scratch=[
            pltpu.VMEM(queries.shape, BF),
            pltpu.VMEM(keys.shape, BF),
            pltpu.VMEM(values.shape, BF),
            pltpu.SemaphoreType.DMA((3,)),
        ],
        space=pltpu.HBM, vmem=62 * 1024 * 1024,
    )
    sorted_ = lax.all_to_all(packed, "head", 0, 0)
    kv = call(
        functools.partial(unpack_kernel, kv_rows), struct((heads, 2, n_keys, DH), BF), sorted_
    )
    query = call(
        functools.partial(spread_kernel, kv_rows), struct((n_y, heads, period, DH), BF), sorted_
    )

    pair_left = shift(kv, "x", 1)
    pair_right = shift(kv, "x", -1)
    query_all = lax.all_to_all(query, "y", 0, 0)
    cut = (heads + 1) // 2
    far_low, far_high = (
        shift(
            call(
                functools.partial(take_kernel, first),
                struct((count,) + kv.shape[1:], BF),
                pair,
                flops=2 * 10**10,
            ),
            "x",
            by,
        )
        for pair, first, count, by in ((pair_left, 0, cut, 1), (pair_right, cut, heads - cut, -1))
    )

    x = lax.axis_index("x")
    places = jnp.stack([x, (x + n_x - 1) % n_x, (x + 1) % n_x, (x + 2) % n_x])
    owned = (places[:, None] * n_y + lax.axis_index("y")) * blocks + jnp.arange(blocks)
    owned = owned.reshape(-1)
    listed = jnp.arange(mask_cols.shape[1])[None, :] < mask_counts[:, None]
    hit = (mask_cols[:, :, None] == owned) & listed[:, :, None]
    bias = jnp.where(jnp.any(hit, axis=1), 0.0, CLOSED).astype(F32)
    bias = jnp.repeat(bias, qt, axis=0)

    flops = 4 * rows * n_keys * heads * DH
    state = call(
        functools.partial(attend_kernel, blocks, tokens),
        (struct((heads, rows, DH), F32),) * 3,
        query_all,
        bias,
        kv,
        pair_left,
        pair_right,
        light=True,
    )
    part = call(
        functools.partial(last_kernel, blocks, tokens, 3),
        struct((n_y * n_z, heads * qb + 1, qt, DH), BF),
        query_all,
        bias,
        far_low,
        far_high,
        *state,
        flops=flops,
    )
    part = lax.all_to_all(part, ("y", "head"), 0, 0)
    return call(functools.partial(merge_kernel, n_y), struct((qb, qt, d), BF), part)


def solution(mesh):
    cfg, head, kv = (mesh.shape[name] for name in ("cfg", "head", "kv"))
    n_x = 4
    fine = Mesh(mesh.devices.reshape(cfg, head, n_x, kv // n_x), ("cfg", "head", "x", "y"))
    token = P(("cfg", "head"), ("x", "y"), None)
    block = P(("cfg", "x", "y"), "head", None)
    return jax.shard_map(
        local,
        mesh=fine,
        in_specs=(token, block, block, P(), P()),
        out_specs=token,
        check_vma=False,
    )
```

```python
import functools

import jax
import jax.numpy as jnp
from jax import lax
from jax.experimental import pallas as pl
from jax.experimental.pallas import tpu as pltpu
from jax.sharding import Mesh
from jax.sharding import PartitionSpec as P

DH = 128
SCALE = 1.4426950408889634 / DH**0.5
CLOSED = -1e30
VMEM_LIMIT = 20 * 1024 * 1024
BF = jnp.bfloat16
F32 = jnp.float32


def pack_kernel(q_hbm, k_hbm, v_hbm, out_ref, q_ref, k_ref, v_ref, sems):
    copies = [
        pltpu.make_async_copy(k_hbm, k_ref, sems.at[0]),
        pltpu.make_async_copy(v_hbm, v_ref, sems.at[1]),
        pltpu.make_async_copy(q_hbm, q_ref, sems.at[2]),
    ]
    for copy in copies:
        copy.start()
    n_z, heads = out_ref.shape[:2]
    blocks, tokens, _ = k_ref.shape
    qb, qt, _ = q_ref.shape
    for part, ref in enumerate((k_ref, v_ref)):
        copies[part].wait()
        for z in range(n_z):
            for h in range(heads):
                columns = pl.ds((z * heads + h) * DH, DH)
                for b in range(blocks):
                    rows = pl.ds((part * blocks + b) * tokens, tokens)
                    out_ref[z, h, rows, :] = ref[b, :, columns]
    copies[2].wait()
    queries = jnp.concatenate([q_ref[i].astype(F32) for i in range(qb)], axis=0).astype(BF)
    for z in range(n_z):
        for h in range(heads):
            first = (z * heads + h) * DH
            out_ref[z, h, pl.ds(2 * blocks * tokens, qb * qt), :] = queries[:, first : first + DH]


def unpack_kernel(kv_rows, sorted_ref, kv_ref):
    n_z, heads, _, _ = sorted_ref.shape
    for h in range(heads):
        for z in range(n_z):
            for part in range(2):
                rows = sorted_ref[z, h, pl.ds(part * kv_rows, kv_rows), :]
                kv_ref[h, part, pl.ds(z * kv_rows, kv_rows), :] = rows


def spread_kernel(kv_rows, sorted_ref, q_ref):
    n_z, heads, rows, _ = sorted_ref.shape
    for h in range(heads):
        query = jnp.concatenate(
            [sorted_ref[z, h, pl.ds(2 * kv_rows, rows - 2 * kv_rows), :].astype(F32) for z in range(n_z)],
            axis=0,
        ).astype(BF)
        for to in range(q_ref.shape[0]):
            q_ref[to, h] = query


def take_kernel(first, pair_ref, out_ref):
    out_ref[...] = pair_ref[pl.ds(first, out_ref.shape[0])]


def block_bias(bias_ref, piece, blocks, tokens, keys):
    place = piece * blocks
    block = lax.broadcasted_iota(jnp.int32, (bias_ref.shape[0], keys), 1) // tokens % blocks
    bias = jnp.broadcast_to(bias_ref[:, place : place + 1], block.shape)
    for b in range(1, blocks):
        bias = jnp.where(block == b, bias_ref[:, place + b : place + b + 1], bias)
    return bias


def scores_of(query, key, bias):
    s = lax.dot_general(query, key, (((1,), (1,)), ((), ())), preferred_element_type=F32)
    period, keys = bias.shape
    return (s.reshape(-1, period, keys) + bias[None]).reshape(s.shape)


def weigh(scores, top, value):
    weight = jnp.exp2((scores - top) * SCALE).astype(BF)
    ones = jnp.ones(value.shape, BF)
    return jnp.dot(weight, jnp.concatenate([value, ones], axis=1), preferred_element_type=F32)


def attend_kernel(blocks, tokens, q_ref, bias_ref, *refs):
    pieces, (top_ref, total_ref, sum_ref) = refs[:-3], refs[-3:]
    n_to, heads, period, _ = q_ref.shape
    rows, keys = n_to * period, pieces[0].shape[2]
    bias = [block_bias(bias_ref, i, blocks, tokens, keys) for i in range(len(pieces))]
    for h in range(heads):
        query = q_ref[:, h].reshape(rows, DH)
        scores = [scores_of(query, ref[h, 0], item) for ref, item in zip(pieces, bias, strict=True)]
        top = jnp.max(functools.reduce(jnp.maximum, scores), axis=1, keepdims=True)
        both = jnp.zeros((rows, 2 * DH), F32)
        for s, ref in zip(scores, pieces, strict=True):
            both = both + weigh(s, top, ref[h, 1])
        top_ref[h] = jnp.broadcast_to(top, (rows, DH))
        sum_ref[h] = both[:, :DH]
        total_ref[h] = both[:, DH:]


def last_kernel(blocks, tokens, piece, q_ref, bias_ref, low_ref, high_ref, top_ref, total_ref, sum_ref, out_ref):
    n_to, heads, period, _ = q_ref.shape
    rows, keys = n_to * period, low_ref.shape[2]
    bias = block_bias(bias_ref, piece, blocks, tokens, keys)
    lane = lax.broadcasted_iota(jnp.int32, (rows, DH), 1)
    tops = jnp.zeros((rows, DH), F32)
    totals = jnp.ones((rows, DH), F32)
    n_dest, parts, qt, _ = out_ref.shape
    qb = parts // heads
    own = qb * qt
    for h in range(heads):
        cut = low_ref.shape[0]
        pair = low_ref.at[h] if h < cut else high_ref.at[h - cut]
        scores = scores_of(q_ref[:, h].reshape(rows, DH), pair[0], bias)
        before = top_ref[h]
        top = jnp.maximum(jnp.max(scores, axis=1, keepdims=True), before)
        fade = jnp.exp2((before - top) * SCALE)
        both = weigh(scores, jnp.concatenate([top] * (keys // DH), axis=1), pair[1])
        total = total_ref[h] * fade + both[:, DH:]
        out = (sum_ref[h] * fade + both[:, :DH]) / total
        out = out.reshape(n_dest, own, DH)
        for b in range(qb):
            out_ref[:, h * qb + b] = out[:, b * qt : (b + 1) * qt].astype(BF)
        tops = jnp.where(lane == h, top, tops)
        totals = jnp.where(lane == h, total, totals)
    lse = tops * (1.0 / DH**0.5) + jnp.log(totals)
    high = lse.astype(BF).astype(F32)
    rest = lse - high
    middle = rest.astype(BF).astype(F32)
    stats = high + pltpu.roll(middle, heads, 1) + pltpu.roll(rest - middle, 2 * heads, 1)
    stats = stats.reshape(n_dest, own, DH)
    joined = stats[:, :qt]
    for b in range(1, qb):
        joined = joined + pltpu.roll(stats, b * (DH // qb), 2)[:, b * qt : (b + 1) * qt]
    out_ref[:, heads * qb] = joined.astype(BF)


def merge_kernel(n_from, part_ref, out_ref):
    n_z = part_ref.shape[0] // n_from
    qb, qt, _ = out_ref.shape
    heads = part_ref.shape[1] // qb

    stats = part_ref[:, heads * qb].astype(F32).reshape(n_from, n_z, qt, DH)
    lse = stats + pltpu.roll(stats, DH - heads, 3) + pltpu.roll(stats, DH - 2 * heads, 3)
    weight = jnp.exp(lse - jnp.max(lse, axis=0, keepdims=True))
    weight = weight / jnp.sum(weight, axis=0, keepdims=True)
    for h in range(heads):
        summed = jnp.zeros((n_z, qb * qt, DH), F32)
        for y in range(n_from):
            lanes = [b * (DH // qb) + h for b in range(qb)]
            factor = jnp.concatenate([weight[y, :, :, i : i + 1] for i in lanes], axis=1)
            out = [part_ref[pl.ds(y * n_z, n_z), h * qb + b].astype(F32) for b in range(qb)]
            summed = summed + jnp.concatenate(out, axis=1) * factor
        for z in range(n_z):
            for b in range(qb):
                rows = summed[z, b * qt : (b + 1) * qt]
                out_ref[b, :, pl.ds((z * heads + h) * DH, DH)] = rows.astype(BF)


def call(kernel, out_shape, *args, flops=0, light=False, scratch=(), space=pltpu.VMEM, vmem=VMEM_LIMIT):
    whole = pl.BlockSpec(memory_space=pltpu.VMEM)
    size = sum(a.size * a.dtype.itemsize for a in args)
    size += sum(o.size * o.dtype.itemsize for o in jax.tree.leaves(out_shape))
    if light:
        size = 0
    return pl.pallas_call(
        kernel,
        out_shape=out_shape,
        in_specs=[pl.BlockSpec(memory_space=space)] * len(args),
        out_specs=jax.tree.map(lambda _: whole, out_shape),
        scratch_shapes=list(scratch),
        compiler_params=pltpu.CompilerParams(vmem_limit_bytes=vmem),
        cost_estimate=pl.CostEstimate(flops=flops, bytes_accessed=size, transcendentals=0),
    )(*args)


def shift(block, axis, by):
    count = lax.axis_size(axis)
    return lax.ppermute(block, axis, [(i, (i + by) % count) for i in range(count)])


def local(queries, keys, values, mask_cols, mask_counts):
    n_z, n_x, n_y = lax.axis_size("head"), lax.axis_size("x"), lax.axis_size("y")
    qb, qt, d = queries.shape
    blocks, tokens, _ = keys.shape
    heads = d // n_z // DH
    kv_rows = blocks * tokens
    own = qb * qt
    period = n_z * own
    rows = n_y * period
    n_keys = n_z * kv_rows
    struct = jax.ShapeDtypeStruct

    packed = call(
        pack_kernel,
        struct((n_z, heads, 2 * kv_rows + own, DH), BF),
        queries,
        keys,
        values,
        scratch=[
            pltpu.VMEM(queries.shape, BF),
            pltpu.VMEM(keys.shape, BF),
            pltpu.VMEM(values.shape, BF),
            pltpu.SemaphoreType.DMA((3,)),
        ],
        space=pltpu.HBM, vmem=62 * 1024 * 1024,
    )
    sorted_ = lax.all_to_all(packed, "head", 0, 0)
    kv = call(
        functools.partial(unpack_kernel, kv_rows), struct((heads, 2, n_keys, DH), BF), sorted_
    )
    query = call(
        functools.partial(spread_kernel, kv_rows), struct((n_y, heads, period, DH), BF), sorted_
    )

    pair_left = shift(kv, "x", 1)
    pair_right = shift(kv, "x", -1)
    query_all = lax.all_to_all(query, "y", 0, 0)
    cut = (heads + 1) // 2
    far_low, far_high = (
        shift(
            call(
                functools.partial(take_kernel, first),
                struct((count,) + kv.shape[1:], BF),
                pair,
                flops=2 * 10**10,
            ),
            "x",
            by,
        )
        for pair, first, count, by in ((pair_left, 0, cut, 1), (pair_right, cut, heads - cut, -1))
    )

    x = lax.axis_index("x")
    places = jnp.stack([x, (x + n_x - 1) % n_x, (x + 1) % n_x, (x + 2) % n_x])
    owned = (places[:, None] * n_y + lax.axis_index("y")) * blocks + jnp.arange(blocks)
    owned = owned.reshape(-1)
    listed = jnp.arange(mask_cols.shape[1])[None, :] < mask_counts[:, None]
    hit = (mask_cols[:, :, None] == owned) & listed[:, :, None]
    bias = jnp.where(jnp.any(hit, axis=1), 0.0, CLOSED).astype(F32)
    bias = jnp.repeat(bias, qt, axis=0)

    flops = 4 * rows * n_keys * heads * DH
    state = call(
        functools.partial(attend_kernel, blocks, tokens),
        (struct((heads, rows, DH), F32),) * 3,
        query_all,
        bias,
        kv,
        pair_left,
        pair_right,
        light=True,
    )
    part = call(
        functools.partial(last_kernel, blocks, tokens, 3),
        struct((n_y * n_z, heads * qb + 1, qt, DH), BF),
        query_all,
        bias,
        far_low,
        far_high,
        *state,
        flops=flops,
    )
    part = lax.all_to_all(part, ("y", "head"), 0, 0)
    return call(functools.partial(merge_kernel, n_y), struct((qb, qt, d), BF), part)


def solution(mesh):
    cfg, head, kv = (mesh.shape[name] for name in ("cfg", "head", "kv"))
    n_x = 4
    fine = Mesh(mesh.devices.reshape(cfg, head, n_x, kv // n_x), ("cfg", "head", "x", "y"))
    token = P(("cfg", "head"), ("x", "y"), None)
    block = P(("cfg", "x", "y"), "head", None)
    return jax.shard_map(
        local,
        mesh=fine,
        in_specs=(token, block, block, P(), P()),
        out_specs=token,
        check_vma=False,
    )
```

```python
import functools

import jax
import jax.numpy as jnp
from jax import lax
from jax.experimental import pallas as pl
from jax.experimental.pallas import tpu as pltpu
from jax.sharding import Mesh
from jax.sharding import PartitionSpec as P

DH = 128
SCALE = 1.4426950408889634 / DH**0.5
CLOSED = -1e30
VMEM_LIMIT = 20 * 1024 * 1024
BF = jnp.bfloat16
F32 = jnp.float32


def pack_kernel(q_hbm, k_hbm, v_hbm, out_ref, q_ref, k_ref, v_ref, sems):
    copies = [
        pltpu.make_async_copy(k_hbm, k_ref, sems.at[0]),
        pltpu.make_async_copy(v_hbm, v_ref, sems.at[1]),
        pltpu.make_async_copy(q_hbm, q_ref, sems.at[2]),
    ]
    for copy in copies:
        copy.start()
    n_z, heads = out_ref.shape[:2]
    blocks, tokens, _ = k_ref.shape
    qb, qt, _ = q_ref.shape
    for part, ref in enumerate((k_ref, v_ref)):
        copies[part].wait()
        for z in range(n_z):
            for h in range(heads):
                columns = pl.ds((z * heads + h) * DH, DH)
                for b in range(blocks):
                    rows = pl.ds((part * blocks + b) * tokens, tokens)
                    out_ref[z, h, rows, :] = ref[b, :, columns]
    copies[2].wait()
    queries = jnp.concatenate([q_ref[i].astype(F32) for i in range(qb)], axis=0).astype(BF)
    for z in range(n_z):
        for h in range(heads):
            first = (z * heads + h) * DH
            out_ref[z, h, pl.ds(2 * blocks * tokens, qb * qt), :] = queries[:, first : first + DH]


def unpack_kernel(kv_rows, sorted_ref, kv_ref):
    n_z, heads, _, _ = sorted_ref.shape
    for h in range(heads):
        for z in range(n_z):
            for part in range(2):
                rows = sorted_ref[z, h, pl.ds(part * kv_rows, kv_rows), :]
                kv_ref[h, part, pl.ds(z * kv_rows, kv_rows), :] = rows


def spread_kernel(kv_rows, sorted_ref, q_ref):
    n_z, heads, rows, _ = sorted_ref.shape
    for h in range(heads):
        query = jnp.concatenate(
            [sorted_ref[z, h, pl.ds(2 * kv_rows, rows - 2 * kv_rows), :].astype(F32) for z in range(n_z)],
            axis=0,
        ).astype(BF)
        for to in range(q_ref.shape[0]):
            q_ref[to, h] = query


def take_kernel(first, pair_ref, out_hbm, sem):
    copy = pltpu.make_async_copy(pair_ref.at[pl.ds(first, out_hbm.shape[0])], out_hbm, sem.at[0])
    copy.start()
    copy.wait()


def block_bias(bias_ref, piece, blocks, tokens, keys):
    place = piece * blocks
    block = lax.broadcasted_iota(jnp.int32, (bias_ref.shape[0], keys), 1) // tokens % blocks
    bias = jnp.broadcast_to(bias_ref[:, place : place + 1], block.shape)
    for b in range(1, blocks):
        bias = jnp.where(block == b, bias_ref[:, place + b : place + b + 1], bias)
    return bias


def scores_of(query, key, bias):
    s = lax.dot_general(query, key, (((1,), (1,)), ((), ())), preferred_element_type=F32)
    period, keys = bias.shape
    return (s.reshape(-1, period, keys) + bias[None]).reshape(s.shape)


def weigh(scores, top, value):
    weight = jnp.exp2((scores - top) * SCALE).astype(BF)
    ones = jnp.ones(value.shape, BF)
    return jnp.dot(weight, jnp.concatenate([value, ones], axis=1), preferred_element_type=F32)


def attend_kernel(blocks, tokens, q_ref, bias_ref, *refs):
    pieces, (top_ref, total_ref, sum_ref) = refs[:-3], refs[-3:]
    n_to, heads, period, _ = q_ref.shape
    rows, keys = n_to * period, pieces[0].shape[2]
    bias = [block_bias(bias_ref, i, blocks, tokens, keys) for i in range(len(pieces))]
    for h in range(heads):
        query = q_ref[:, h].reshape(rows, DH)
        scores = [scores_of(query, ref[h, 0], item) for ref, item in zip(pieces, bias, strict=True)]
        top = jnp.max(functools.reduce(jnp.maximum, scores), axis=1, keepdims=True)
        both = jnp.zeros((rows, 2 * DH), F32)
        for s, ref in zip(scores, pieces, strict=True):
            both = both + weigh(s, top, ref[h, 1])
        top_ref[h] = jnp.broadcast_to(top, (rows, DH))
        sum_ref[h] = both[:, :DH]
        total_ref[h] = both[:, DH:]


def last_kernel(blocks, tokens, piece, q_ref, bias_ref, low_ref, high_ref, top_ref, total_ref, sum_ref, out_ref):
    n_to, heads, period, _ = q_ref.shape
    rows, keys = n_to * period, low_ref.shape[2]
    bias = block_bias(bias_ref, piece, blocks, tokens, keys)
    lane = lax.broadcasted_iota(jnp.int32, (rows, DH), 1)
    tops = jnp.zeros((rows, DH), F32)
    totals = jnp.ones((rows, DH), F32)
    n_dest, parts, qt, _ = out_ref.shape
    qb = parts // heads
    own = qb * qt

    def in_place(item):
        item = item.reshape(n_to, n_dest // n_to, own, DH)
        item = jnp.stack([item[n_to - 1 - y] for y in range(n_to)])
        return item.reshape(n_dest, own, DH)

    for h in range(heads):
        cut = low_ref.shape[0]
        pair = low_ref.at[h] if h < cut else high_ref.at[h - cut]
        scores = scores_of(q_ref[:, h].reshape(rows, DH), pair[0], bias)
        before = top_ref[h]
        top = jnp.maximum(jnp.max(scores, axis=1, keepdims=True), before)
        fade = jnp.exp2((before - top) * SCALE)
        both = weigh(scores, jnp.concatenate([top] * (keys // DH), axis=1), pair[1])
        total = total_ref[h] * fade + both[:, DH:]
        out = (sum_ref[h] * fade + both[:, :DH]) / total
        out = in_place(out)
        for b in range(qb):
            out_ref[:, h * qb + b] = out[:, b * qt : (b + 1) * qt].astype(BF)
        tops = jnp.where(lane == h, top, tops)
        totals = jnp.where(lane == h, total, totals)
    lse = tops * (1.0 / DH**0.5) + jnp.log(totals)
    high = lse.astype(BF).astype(F32)
    rest = lse - high
    middle = rest.astype(BF).astype(F32)
    stats = high + pltpu.roll(middle, heads, 1) + pltpu.roll(rest - middle, 2 * heads, 1)
    stats = in_place(stats)
    joined = stats[:, :qt]
    for b in range(1, qb):
        joined = joined + pltpu.roll(stats, b * (DH // qb), 2)[:, b * qt : (b + 1) * qt]
    out_ref[:, heads * qb] = joined.astype(BF)


def merge_kernel(n_from, part_ref, out_ref):
    n_z = part_ref.shape[0] // n_from
    qb, qt, _ = out_ref.shape
    heads = part_ref.shape[1] // qb

    stats = part_ref[:, heads * qb].astype(F32).reshape(n_from, n_z, qt, DH)
    lse = stats + pltpu.roll(stats, DH - heads, 3) + pltpu.roll(stats, DH - 2 * heads, 3)
    weight = jnp.exp(lse - jnp.max(lse, axis=0, keepdims=True))
    weight = weight / jnp.sum(weight, axis=0, keepdims=True)
    for h in range(heads):
        summed = jnp.zeros((n_z, qb * qt, DH), F32)
        for y in range(n_from):
            lanes = [b * (DH // qb) + h for b in range(qb)]
            factor = jnp.concatenate([weight[y, :, :, i : i + 1] for i in lanes], axis=1)
            out = [part_ref[pl.ds(y * n_z, n_z), h * qb + b].astype(F32) for b in range(qb)]
            summed = summed + jnp.concatenate(out, axis=1) * factor
        for z in range(n_z):
            for b in range(qb):
                rows = summed[z, b * qt : (b + 1) * qt]
                out_ref[b, :, pl.ds((z * heads + h) * DH, DH)] = rows.astype(BF)


def call(kernel, out_shape, *args, flops=0, light=False, scratch=(), space=pltpu.VMEM, out_space=pltpu.VMEM, vmem=VMEM_LIMIT):
    whole = pl.BlockSpec(memory_space=out_space)
    size = sum(a.size * a.dtype.itemsize for a in args)
    size += sum(o.size * o.dtype.itemsize for o in jax.tree.leaves(out_shape))
    if light:
        size = 0
    return pl.pallas_call(
        kernel,
        out_shape=out_shape,
        in_specs=[pl.BlockSpec(memory_space=space)] * len(args),
        out_specs=jax.tree.map(lambda _: whole, out_shape),
        scratch_shapes=list(scratch),
        compiler_params=pltpu.CompilerParams(vmem_limit_bytes=vmem),
        cost_estimate=pl.CostEstimate(flops=flops, bytes_accessed=size, transcendentals=0),
    )(*args)


def shift(block, axis, by):
    count = lax.axis_size(axis)
    return lax.ppermute(block, axis, [(i, (i + by) % count) for i in range(count)])


def local(queries, keys, values, mask_cols, mask_counts):
    n_z, n_x, n_y = lax.axis_size("head"), lax.axis_size("x"), lax.axis_size("y")
    qb, qt, d = queries.shape
    blocks, tokens, _ = keys.shape
    heads = d // n_z // DH
    kv_rows = blocks * tokens
    own = qb * qt
    period = n_z * own
    rows = n_y * period
    n_keys = n_z * kv_rows
    struct = jax.ShapeDtypeStruct

    packed = call(
        pack_kernel,
        struct((n_z, heads, 2 * kv_rows + own, DH), BF),
        queries,
        keys,
        values,
        scratch=[
            pltpu.VMEM(queries.shape, BF),
            pltpu.VMEM(keys.shape, BF),
            pltpu.VMEM(values.shape, BF),
            pltpu.SemaphoreType.DMA((3,)),
        ],
        space=pltpu.HBM, vmem=62 * 1024 * 1024,
    )
    sorted_ = lax.all_to_all(packed, "head", 0, 0)
    kv = call(
        functools.partial(unpack_kernel, kv_rows), struct((heads, 2, n_keys, DH), BF), sorted_
    )
    query = call(
        functools.partial(spread_kernel, kv_rows), struct((n_y, heads, period, DH), BF), sorted_
    )

    pair_left = shift(kv, "x", 1)
    pair_right = shift(kv, "x", -1)
    query_all = lax.all_to_all(query, "y", 0, 0, axis_index_groups=[list(range(n_y))[::-1]])
    cut = (heads + 1) // 2
    far_low, far_high = (
        shift(
            call(
                functools.partial(take_kernel, first),
                struct((count,) + kv.shape[1:], BF),
                pair,
                flops=2 * 10**10,
                scratch=[pltpu.SemaphoreType.DMA((1,))],
                out_space=pltpu.HBM,
            ),
            "x",
            by,
        )
        for pair, first, count, by in ((pair_left, 0, cut, 1), (pair_right, cut, heads - cut, -1))
    )

    x = lax.axis_index("x")
    places = jnp.stack([x, (x + n_x - 1) % n_x, (x + 1) % n_x, (x + 2) % n_x])
    owned = (places[:, None] * n_y + lax.axis_index("y")) * blocks + jnp.arange(blocks)
    owned = owned.reshape(-1)
    listed = jnp.arange(mask_cols.shape[1])[None, :] < mask_counts[:, None]
    hit = (mask_cols[:, :, None] == owned) & listed[:, :, None]
    bias = jnp.where(jnp.any(hit, axis=1), 0.0, CLOSED).astype(F32)
    bias = jnp.repeat(bias, qt, axis=0)

    flops = 4 * rows * n_keys * heads * DH
    state = call(
        functools.partial(attend_kernel, blocks, tokens),
        (struct((heads, rows, DH), F32),) * 3,
        query_all,
        bias,
        kv,
        pair_left,
        pair_right,
        light=True,
    )
    part = call(
        functools.partial(last_kernel, blocks, tokens, 3),
        struct((n_y * n_z, heads * qb + 1, qt, DH), BF),
        query_all,
        bias,
        far_low,
        far_high,
        *state,
        flops=flops,
    )
    part = lax.all_to_all(part, ("y", "head"), 0, 0)
    return call(functools.partial(merge_kernel, n_y), struct((qb, qt, d), BF), part)


def solution(mesh):
    cfg, head, kv = (mesh.shape[name] for name in ("cfg", "head", "kv"))
    n_x = 4
    fine = Mesh(mesh.devices.reshape(cfg, head, n_x, kv // n_x), ("cfg", "head", "x", "y"))
    token = P(("cfg", "head"), ("x", "y"), None)
    block = P(("cfg", "x", "y"), "head", None)
    return jax.shard_map(
        local,
        mesh=fine,
        in_specs=(token, block, block, P(), P()),
        out_specs=token,
        check_vma=False,
    )
```

```python
import functools

import jax
import jax.numpy as jnp
from jax import lax
from jax.experimental import pallas as pl
from jax.experimental.pallas import tpu as pltpu
from jax.sharding import Mesh
from jax.sharding import PartitionSpec as P

DH = 128
SCALE = 1.4426950408889634 / DH**0.5
CLOSED = -1e30
VMEM_LIMIT = 20 * 1024 * 1024
BF = jnp.bfloat16
F32 = jnp.float32


def pack_kernel(q_hbm, k_hbm, v_hbm, out_ref, q_ref, k_ref, v_ref, sems):
    copies = [
        pltpu.make_async_copy(k_hbm, k_ref, sems.at[0]),
        pltpu.make_async_copy(v_hbm, v_ref, sems.at[1]),
        pltpu.make_async_copy(q_hbm, q_ref, sems.at[2]),
    ]
    for copy in copies:
        copy.start()
    n_z, heads = out_ref.shape[:2]
    blocks, tokens, _ = k_ref.shape
    qb, qt, _ = q_ref.shape
    for part, ref in enumerate((k_ref, v_ref)):
        copies[part].wait()
        for z in range(n_z):
            for h in range(heads):
                columns = pl.ds((z * heads + h) * DH, DH)
                for b in range(blocks):
                    rows = pl.ds((part * blocks + b) * tokens, tokens)
                    out_ref[z, h, rows, :] = ref[b, :, columns]
    copies[2].wait()
    queries = jnp.concatenate([q_ref[i].astype(F32) for i in range(qb)], axis=0).astype(BF)
    for z in range(n_z):
        for h in range(heads):
            first = (z * heads + h) * DH
            out_ref[z, h, pl.ds(2 * blocks * tokens, qb * qt), :] = queries[:, first : first + DH]


def unpack_kernel(kv_rows, sorted_ref, kv_ref):
    n_z, heads, _, _ = sorted_ref.shape
    for h in range(heads):
        for z in range(n_z):
            for part in range(2):
                rows = sorted_ref[z, h, pl.ds(part * kv_rows, kv_rows), :]
                kv_ref[h, part, pl.ds(z * kv_rows, kv_rows), :] = rows


def spread_kernel(kv_rows, sorted_ref, q_ref):
    n_z, heads, rows, _ = sorted_ref.shape
    for h in range(heads):
        query = jnp.concatenate(
            [sorted_ref[z, h, pl.ds(2 * kv_rows, rows - 2 * kv_rows), :].astype(F32) for z in range(n_z)],
            axis=0,
        ).astype(BF)
        for to in range(q_ref.shape[0]):
            q_ref[to, h] = query


def take_kernel(first, pair_ref, out_hbm, sem):
    copy = pltpu.make_async_copy(pair_ref.at[pl.ds(first, out_hbm.shape[0])], out_hbm, sem.at[0])
    copy.start()
    copy.wait()


def block_bias(bias_ref, piece, blocks, tokens, keys):
    place = piece * blocks
    block = lax.broadcasted_iota(jnp.int32, (bias_ref.shape[0], keys), 1) // tokens % blocks
    bias = jnp.broadcast_to(bias_ref[:, place : place + 1], block.shape)
    for b in range(1, blocks):
        bias = jnp.where(block == b, bias_ref[:, place + b : place + b + 1], bias)
    return bias


def scores_of(query, key, bias):
    s = lax.dot_general(query, key, (((1,), (1,)), ((), ())), preferred_element_type=F32)
    period, keys = bias.shape
    return (s.reshape(-1, period, keys) + bias[None]).reshape(s.shape)


def weigh(scores, top, value):
    weight = jnp.exp2((scores - top) * SCALE).astype(BF)
    ones = jnp.ones(value.shape, BF)
    return jnp.dot(weight, jnp.concatenate([value, ones], axis=1), preferred_element_type=F32)


def attend_kernel(blocks, tokens, q_ref, bias_ref, *refs):
    pieces, (top_ref, total_ref, sum_ref) = refs[:-3], refs[-3:]
    n_to, heads, period, _ = q_ref.shape
    rows, keys = n_to * period, pieces[0].shape[2]
    bias = [block_bias(bias_ref, i, blocks, tokens, keys) for i in range(len(pieces))]
    for h in range(heads):
        query = q_ref[:, h].reshape(rows, DH)
        scores = [scores_of(query, ref[h, 0], item) for ref, item in zip(pieces, bias, strict=True)]
        top = jnp.max(functools.reduce(jnp.maximum, scores), axis=1, keepdims=True)
        both = jnp.zeros((rows, 2 * DH), F32)
        for s, ref in zip(scores, pieces, strict=True):
            both = both + weigh(s, top, ref[h, 1])
        top_ref[h] = jnp.broadcast_to(top, (rows, DH))
        sum_ref[h] = both[:, :DH]
        total_ref[h] = both[:, DH:]


def last_kernel(blocks, tokens, piece, q_ref, bias_ref, low_ref, high_ref, top_ref, total_ref, sum_ref, out_ref):
    n_to, heads, period, _ = q_ref.shape
    rows, keys = n_to * period, low_ref.shape[2]
    bias = block_bias(bias_ref, piece, blocks, tokens, keys)
    lane = lax.broadcasted_iota(jnp.int32, (rows, DH), 1)
    tops = jnp.zeros((rows, DH), F32)
    totals = jnp.ones((rows, DH), F32)
    n_dest, parts, qt, _ = out_ref.shape
    qb = parts // heads
    own = qb * qt

    def in_place(item):
        item = item.reshape(n_to, n_dest // n_to, own, DH)
        item = jnp.stack([item[n_to - 1 - y] for y in range(n_to)])
        return item.reshape(n_dest, own, DH)

    for h in range(heads):
        cut = low_ref.shape[0]
        pair = low_ref.at[h] if h < cut else high_ref.at[h - cut]
        scores = scores_of(q_ref[:, h].reshape(rows, DH), pair[0], bias)
        before = top_ref[h]
        top = jnp.maximum(jnp.max(scores, axis=1, keepdims=True), before)
        fade = jnp.exp2((before - top) * SCALE)
        both = weigh(scores, jnp.concatenate([top] * (keys // DH), axis=1), pair[1])
        total = total_ref[h] * fade + both[:, DH:]
        inverse = pl.reciprocal(total, approx=True)
        inverse = inverse * (2.0 - total * inverse)
        out = (sum_ref[h] * fade + both[:, :DH]) * inverse
        out = in_place(out)
        for b in range(qb):
            out_ref[:, h * qb + b] = out[:, b * qt : (b + 1) * qt].astype(BF)
        tops = jnp.where(lane == h, top, tops)
        totals = jnp.where(lane == h, total, totals)
    lse = tops * (1.0 / DH**0.5) + jnp.log(totals)
    high = lse.astype(BF).astype(F32)
    rest = lse - high
    middle = rest.astype(BF).astype(F32)
    stats = high + pltpu.roll(middle, heads, 1) + pltpu.roll(rest - middle, 2 * heads, 1)
    stats = in_place(stats)
    joined = stats[:, :qt]
    for b in range(1, qb):
        joined = joined + pltpu.roll(stats, b * (DH // qb), 2)[:, b * qt : (b + 1) * qt]
    out_ref[:, heads * qb] = joined.astype(BF)


def merge_kernel(n_from, part_ref, out_ref):
    n_z = part_ref.shape[0] // n_from
    qb, qt, _ = out_ref.shape
    heads = part_ref.shape[1] // qb

    stats = part_ref[:, heads * qb].astype(F32).reshape(n_from, n_z, qt, DH)
    lse = stats + pltpu.roll(stats, DH - heads, 3) + pltpu.roll(stats, DH - 2 * heads, 3)
    weight = jnp.exp(lse - jnp.max(lse, axis=0, keepdims=True))
    weight = weight * (1.0 / jnp.sum(weight, axis=0, keepdims=True))
    for h in range(heads):
        summed = jnp.zeros((n_z, qb * qt, DH), F32)
        for y in range(n_from):
            lanes = [b * (DH // qb) + h for b in range(qb)]
            factor = jnp.concatenate([weight[y, :, :, i : i + 1] for i in lanes], axis=1)
            out = [part_ref[pl.ds(y * n_z, n_z), h * qb + b].astype(F32) for b in range(qb)]
            summed = summed + jnp.concatenate(out, axis=1) * factor
        for z in range(n_z):
            for b in range(qb):
                rows = summed[z, b * qt : (b + 1) * qt]
                out_ref[b, :, pl.ds((z * heads + h) * DH, DH)] = rows.astype(BF)


def call(kernel, out_shape, *args, flops=0, light=False, scratch=(), space=pltpu.VMEM, out_space=pltpu.VMEM, vmem=VMEM_LIMIT):
    whole = pl.BlockSpec(memory_space=out_space)
    size = sum(a.size * a.dtype.itemsize for a in args)
    size += sum(o.size * o.dtype.itemsize for o in jax.tree.leaves(out_shape))
    if light:
        size = 0
    return pl.pallas_call(
        kernel,
        out_shape=out_shape,
        in_specs=[pl.BlockSpec(memory_space=space)] * len(args),
        out_specs=jax.tree.map(lambda _: whole, out_shape),
        scratch_shapes=list(scratch),
        compiler_params=pltpu.CompilerParams(vmem_limit_bytes=vmem),
        cost_estimate=pl.CostEstimate(flops=flops, bytes_accessed=size, transcendentals=0),
    )(*args)


def shift(block, axis, by):
    count = lax.axis_size(axis)
    return lax.ppermute(block, axis, [(i, (i + by) % count) for i in range(count)])


def local(queries, keys, values, mask_cols, mask_counts):
    n_z, n_x, n_y = lax.axis_size("head"), lax.axis_size("x"), lax.axis_size("y")
    qb, qt, d = queries.shape
    blocks, tokens, _ = keys.shape
    heads = d // n_z // DH
    kv_rows = blocks * tokens
    own = qb * qt
    period = n_z * own
    rows = n_y * period
    n_keys = n_z * kv_rows
    struct = jax.ShapeDtypeStruct

    packed = call(
        pack_kernel,
        struct((n_z, heads, 2 * kv_rows + own, DH), BF),
        queries,
        keys,
        values,
        scratch=[
            pltpu.VMEM(queries.shape, BF),
            pltpu.VMEM(keys.shape, BF),
            pltpu.VMEM(values.shape, BF),
            pltpu.SemaphoreType.DMA((3,)),
        ],
        space=pltpu.HBM, vmem=62 * 1024 * 1024,
    )
    sorted_ = lax.all_to_all(packed, "head", 0, 0)
    kv = call(
        functools.partial(unpack_kernel, kv_rows), struct((heads, 2, n_keys, DH), BF), sorted_
    )
    query = call(
        functools.partial(spread_kernel, kv_rows), struct((n_y, heads, period, DH), BF), sorted_
    )

    pair_left = shift(kv, "x", 1)
    pair_right = shift(kv, "x", -1)
    query_all = lax.all_to_all(query, "y", 0, 0, axis_index_groups=[list(range(n_y))[::-1]])
    cut = (heads + 1) // 2
    far_low, far_high = (
        shift(
            call(
                functools.partial(take_kernel, first),
                struct((count,) + kv.shape[1:], BF),
                pair,
                flops=2 * 10**10,
                scratch=[pltpu.SemaphoreType.DMA((1,))],
                out_space=pltpu.HBM,
            ),
            "x",
            by,
        )
        for pair, first, count, by in ((pair_left, 0, cut, 1), (pair_right, cut, heads - cut, -1))
    )

    x = lax.axis_index("x")
    places = jnp.stack([x, (x + n_x - 1) % n_x, (x + 1) % n_x, (x + 2) % n_x])
    owned = (places[:, None] * n_y + lax.axis_index("y")) * blocks + jnp.arange(blocks)
    owned = owned.reshape(-1)
    listed = jnp.arange(mask_cols.shape[1])[None, :] < mask_counts[:, None]
    hit = (mask_cols[:, :, None] == owned) & listed[:, :, None]
    bias = jnp.where(jnp.any(hit, axis=1), 0.0, CLOSED).astype(F32)
    bias = jnp.repeat(bias, qt, axis=0)

    flops = 4 * rows * n_keys * heads * DH
    state = call(
        functools.partial(attend_kernel, blocks, tokens),
        (struct((heads, rows, DH), F32),) * 3,
        query_all,
        bias,
        kv,
        pair_left,
        pair_right,
        light=True,
    )
    part = call(
        functools.partial(last_kernel, blocks, tokens, 3),
        struct((n_y * n_z, heads * qb + 1, qt, DH), BF),
        query_all,
        bias,
        far_low,
        far_high,
        *state,
        flops=flops,
    )
    part = lax.all_to_all(part, ("y", "head"), 0, 0)
    return call(functools.partial(merge_kernel, n_y), struct((qb, qt, d), BF), part)


def solution(mesh):
    cfg, head, kv = (mesh.shape[name] for name in ("cfg", "head", "kv"))
    n_x = 4
    fine = Mesh(mesh.devices.reshape(cfg, head, n_x, kv // n_x), ("cfg", "head", "x", "y"))
    token = P(("cfg", "head"), ("x", "y"), None)
    block = P(("cfg", "x", "y"), "head", None)
    return jax.shard_map(
        local,
        mesh=fine,
        in_specs=(token, block, block, P(), P()),
        out_specs=token,
        check_vma=False,
    )
```

```python
import functools

import jax
import jax.numpy as jnp
from jax import lax
from jax.experimental import pallas as pl
from jax.experimental.pallas import tpu as pltpu
from jax.sharding import Mesh
from jax.sharding import PartitionSpec as P

DH = 128
SCALE = 1.4426950408889634 / DH**0.5
CLOSED = -1e30
VMEM_LIMIT = 20 * 1024 * 1024
BF = jnp.bfloat16
F32 = jnp.float32


def pack_kernel(q_hbm, k_hbm, v_hbm, out_ref, q_ref, k_ref, v_ref, sems):
    copies = [
        pltpu.make_async_copy(k_hbm, k_ref, sems.at[0]),
        pltpu.make_async_copy(v_hbm, v_ref, sems.at[1]),
        pltpu.make_async_copy(q_hbm, q_ref, sems.at[2]),
    ]
    for copy in copies:
        copy.start()
    n_z, heads = out_ref.shape[:2]
    blocks, tokens, _ = k_ref.shape
    qb, qt, _ = q_ref.shape
    for part, ref in enumerate((k_ref, v_ref)):
        copies[part].wait()
        for z in range(n_z):
            for h in range(heads):
                columns = pl.ds((z * heads + h) * DH, DH)
                for b in range(blocks):
                    rows = pl.ds((part * blocks + b) * tokens, tokens)
                    out_ref[z, h, rows, :] = ref[b, :, columns]
    copies[2].wait()
    queries = jnp.concatenate([q_ref[i].astype(F32) for i in range(qb)], axis=0).astype(BF)
    for z in range(n_z):
        for h in range(heads):
            first = (z * heads + h) * DH
            out_ref[z, h, pl.ds(2 * blocks * tokens, qb * qt), :] = queries[:, first : first + DH]


def unpack_kernel(kv_rows, sorted_ref, kv_ref):
    n_z, heads, _, _ = sorted_ref.shape
    for h in range(heads):
        for z in range(n_z):
            for part in range(2):
                rows = sorted_ref[z, h, pl.ds(part * kv_rows, kv_rows), :]
                kv_ref[h, part, pl.ds(z * kv_rows, kv_rows), :] = rows


def spread_kernel(kv_rows, sorted_ref, q_ref):
    n_z, heads, rows, _ = sorted_ref.shape
    for h in range(heads):
        query = jnp.concatenate(
            [sorted_ref[z, h, pl.ds(2 * kv_rows, rows - 2 * kv_rows), :].astype(F32) for z in range(n_z)],
            axis=0,
        ).astype(BF)
        for to in range(q_ref.shape[0]):
            q_ref[to, h] = query


def take_kernel(first, pair_ref, out_hbm, sem):
    copy = pltpu.make_async_copy(pair_ref.at[pl.ds(first, out_hbm.shape[0])], out_hbm, sem.at[0])
    copy.start()
    copy.wait()


def block_bias(bias_ref, piece, blocks, tokens, keys):
    place = piece * blocks
    block = lax.broadcasted_iota(jnp.int32, (bias_ref.shape[0], keys), 1) // tokens % blocks
    bias = jnp.broadcast_to(bias_ref[:, place : place + 1], block.shape)
    for b in range(1, blocks):
        bias = jnp.where(block == b, bias_ref[:, place + b : place + b + 1], bias)
    return bias


def scores_of(query, key, bias):
    s = lax.dot_general(query, key, (((1,), (1,)), ((), ())), preferred_element_type=F32)
    period, keys = bias.shape
    return (s.reshape(-1, period, keys) + bias[None]).reshape(s.shape)


def weigh(scores, top, value):
    weight = jnp.exp2((scores - top) * SCALE).astype(BF)
    ones = jnp.ones(value.shape, BF)
    return jnp.dot(weight, jnp.concatenate([value, ones], axis=1), preferred_element_type=F32)


def attend_kernel(blocks, tokens, q_ref, bias_ref, *refs):
    pieces, (top_ref, total_ref, sum_ref) = refs[:-3], refs[-3:]
    n_to, heads, period, _ = q_ref.shape
    rows, keys = n_to * period, pieces[0].shape[2]
    bias = [block_bias(bias_ref, i, blocks, tokens, keys) for i in range(len(pieces))]
    for h in range(heads):
        query = q_ref[:, h].reshape(rows, DH)
        scores = [scores_of(query, ref[h, 0], item) for ref, item in zip(pieces, bias, strict=True)]
        top = jnp.max(functools.reduce(jnp.maximum, scores), axis=1, keepdims=True)
        both = jnp.zeros((rows, 2 * DH), F32)
        for s, ref in zip(scores, pieces, strict=True):
            both = both + weigh(s, top, ref[h, 1])
        top_ref[h] = jnp.broadcast_to(top, (rows, DH))
        sum_ref[h] = both[:, :DH]
        total_ref[h] = both[:, DH:]


def last_kernel(blocks, tokens, piece, q_ref, bias_ref, low_ref, high_ref, top_ref, total_ref, sum_ref, out_ref):
    n_to, heads, period, _ = q_ref.shape
    rows, keys = n_to * period, low_ref.shape[2]
    bias = block_bias(bias_ref, piece, blocks, tokens, keys)
    lane = lax.broadcasted_iota(jnp.int32, (rows, DH), 1)
    tops = jnp.zeros((rows, DH), F32)
    totals = jnp.ones((rows, DH), F32)
    n_dest, parts, qt, _ = out_ref.shape
    qb = parts // heads
    own = qb * qt

    for h in range(heads):
        cut = low_ref.shape[0]
        pair = low_ref.at[h] if h < cut else high_ref.at[h - cut]
        scores = scores_of(q_ref[:, h].reshape(rows, DH), pair[0], bias)
        before = top_ref[h]
        top = jnp.maximum(jnp.max(scores, axis=1, keepdims=True), before)
        fade = jnp.exp2((before - top) * SCALE)
        both = weigh(scores, jnp.concatenate([top] * (keys // DH), axis=1), pair[1])
        total = total_ref[h] * fade + both[:, DH:]
        out = (sum_ref[h] * fade + both[:, :DH]) / total
        out = out.reshape(n_dest, own, DH)
        for b in range(qb):
            out_ref[:, h * qb + b] = out[:, b * qt : (b + 1) * qt].astype(BF)
        tops = jnp.where(lane == h, top, tops)
        totals = jnp.where(lane == h, total, totals)
    lse = tops * (1.0 / DH**0.5) + jnp.log(totals)
    high = lse.astype(BF).astype(F32)
    rest = lse - high
    middle = rest.astype(BF).astype(F32)
    stats = high + pltpu.roll(middle, heads, 1) + pltpu.roll(rest - middle, 2 * heads, 1)
    stats = stats.reshape(n_dest, own, DH)
    joined = stats[:, :qt]
    for b in range(1, qb):
        joined = joined + pltpu.roll(stats, b * (DH // qb), 2)[:, b * qt : (b + 1) * qt]
    out_ref[:, heads * qb] = joined.astype(BF)


def merge_kernel(n_from, part_ref, out_ref):
    n_z = part_ref.shape[0] // n_from
    qb, qt, _ = out_ref.shape
    heads = part_ref.shape[1] // qb

    stats = part_ref[:, heads * qb].astype(F32).reshape(n_from, n_z, qt, DH)
    lse = stats + pltpu.roll(stats, DH - heads, 3) + pltpu.roll(stats, DH - 2 * heads, 3)
    weight = jnp.exp(lse - jnp.max(lse, axis=0, keepdims=True))
    weight = weight / jnp.sum(weight, axis=0, keepdims=True)
    for h in range(heads):
        summed = jnp.zeros((n_z, qb * qt, DH), F32)
        for y in range(n_from):
            lanes = [b * (DH // qb) + h for b in range(qb)]
            factor = jnp.concatenate([weight[y, :, :, i : i + 1] for i in lanes], axis=1)
            out = [part_ref[pl.ds(y * n_z, n_z), h * qb + b].astype(F32) for b in range(qb)]
            summed = summed + jnp.concatenate(out, axis=1) * factor
        for z in range(n_z):
            for b in range(qb):
                rows = summed[z, b * qt : (b + 1) * qt]
                out_ref[b, :, pl.ds((z * heads + h) * DH, DH)] = rows.astype(BF)


def call(kernel, out_shape, *args, flops=0, light=False, scratch=(), space=pltpu.VMEM, out_space=pltpu.VMEM, vmem=VMEM_LIMIT):
    whole = pl.BlockSpec(memory_space=out_space)
    size = sum(a.size * a.dtype.itemsize for a in args)
    size += sum(o.size * o.dtype.itemsize for o in jax.tree.leaves(out_shape))
    if light:
        size = 0
    return pl.pallas_call(
        kernel,
        out_shape=out_shape,
        in_specs=[pl.BlockSpec(memory_space=space)] * len(args),
        out_specs=jax.tree.map(lambda _: whole, out_shape),
        scratch_shapes=list(scratch),
        compiler_params=pltpu.CompilerParams(vmem_limit_bytes=vmem),
        cost_estimate=pl.CostEstimate(flops=flops, bytes_accessed=size, transcendentals=0),
    )(*args)


def shift(block, axis, by):
    count = lax.axis_size(axis)
    return lax.ppermute(block, axis, [(i, (i + by) % count) for i in range(count)])


def local(queries, keys, values, mask_cols, mask_counts):
    n_z, n_x, n_y = lax.axis_size("head"), lax.axis_size("x"), lax.axis_size("y")
    qb, qt, d = queries.shape
    blocks, tokens, _ = keys.shape
    heads = d // n_z // DH
    kv_rows = blocks * tokens
    own = qb * qt
    period = n_z * own
    rows = n_y * period
    n_keys = n_z * kv_rows
    struct = jax.ShapeDtypeStruct

    packed = call(
        pack_kernel,
        struct((n_z, heads, 2 * kv_rows + own, DH), BF),
        queries,
        keys,
        values,
        scratch=[
            pltpu.VMEM(queries.shape, BF),
            pltpu.VMEM(keys.shape, BF),
            pltpu.VMEM(values.shape, BF),
            pltpu.SemaphoreType.DMA((3,)),
        ],
        space=pltpu.HBM, vmem=62 * 1024 * 1024,
    )
    sorted_ = lax.all_to_all(packed, "head", 0, 0)
    kv = call(
        functools.partial(unpack_kernel, kv_rows), struct((heads, 2, n_keys, DH), BF), sorted_
    )
    query = call(
        functools.partial(spread_kernel, kv_rows), struct((n_y, heads, period, DH), BF), sorted_
    )

    pair_left = shift(kv, "x", 1)
    pair_right = shift(kv, "x", -1)
    query_all = lax.all_to_all(query, "y", 0, 0, axis_index_groups=[list(range(n_y))[::-1]])
    cut = (heads + 1) // 2
    far_low, far_high = (
        shift(
            call(
                functools.partial(take_kernel, first),
                struct((count,) + kv.shape[1:], BF),
                pair,
                flops=2 * 10**10,
                scratch=[pltpu.SemaphoreType.DMA((1,))],
                out_space=pltpu.HBM,
            ),
            "x",
            by,
        )
        for pair, first, count, by in ((pair_left, 0, cut, 1), (pair_right, cut, heads - cut, -1))
    )

    x = lax.axis_index("x")
    places = jnp.stack([x, (x + n_x - 1) % n_x, (x + 1) % n_x, (x + 2) % n_x])
    owned = (places[:, None] * n_y + lax.axis_index("y")) * blocks + jnp.arange(blocks)
    owned = owned.reshape(-1)
    listed = jnp.arange(mask_cols.shape[1])[None, :] < mask_counts[:, None]
    hit = (mask_cols[:, :, None] == owned) & listed[:, :, None]
    bias = jnp.where(jnp.any(hit, axis=1), 0.0, CLOSED).astype(F32)
    bias = jnp.repeat(bias, qt, axis=0)

    flops = 4 * rows * n_keys * heads * DH
    state = call(
        functools.partial(attend_kernel, blocks, tokens),
        (struct((heads, rows, DH), F32),) * 3,
        query_all,
        bias,
        kv,
        pair_left,
        pair_right,
        light=True,
    )
    part = call(
        functools.partial(last_kernel, blocks, tokens, 3),
        struct((n_y * n_z, heads * qb + 1, qt, DH), BF),
        query_all,
        bias,
        far_low,
        far_high,
        *state,
        flops=flops,
    )
    order = [y * n_z + z for y in reversed(range(n_y)) for z in range(n_z)]
    part = lax.all_to_all(part, ("y", "head"), 0, 0, axis_index_groups=[order])
    return call(functools.partial(merge_kernel, n_y), struct((qb, qt, d), BF), part)


def solution(mesh):
    cfg, head, kv = (mesh.shape[name] for name in ("cfg", "head", "kv"))
    n_x = 4
    fine = Mesh(mesh.devices.reshape(cfg, head, n_x, kv // n_x), ("cfg", "head", "x", "y"))
    token = P(("cfg", "head"), ("x", "y"), None)
    block = P(("cfg", "x", "y"), "head", None)
    return jax.shard_map(
        local,
        mesh=fine,
        in_specs=(token, block, block, P(), P()),
        out_specs=token,
        check_vma=False,
    )
```

```python
import functools

import jax
import jax.numpy as jnp
from jax import lax
from jax.experimental import pallas as pl
from jax.experimental.pallas import tpu as pltpu
from jax.sharding import Mesh
from jax.sharding import PartitionSpec as P

DH = 128
SCALE = 1.4426950408889634 / DH**0.5
CLOSED = -1e30
VMEM_LIMIT = 20 * 1024 * 1024
BF = jnp.bfloat16
F32 = jnp.float32


def pack_kernel(q_hbm, k_hbm, v_hbm, out_ref, q_ref, k_ref, v_ref, sems):
    copies = [
        pltpu.make_async_copy(k_hbm, k_ref, sems.at[0]),
        pltpu.make_async_copy(v_hbm, v_ref, sems.at[1]),
        pltpu.make_async_copy(q_hbm, q_ref, sems.at[2]),
    ]
    for copy in copies:
        copy.start()
    n_z, heads = out_ref.shape[:2]
    blocks, tokens, _ = k_ref.shape
    qb, qt, _ = q_ref.shape
    for part, ref in enumerate((k_ref, v_ref)):
        copies[part].wait()
        for z in range(n_z):
            for h in range(heads):
                columns = pl.ds((z * heads + h) * DH, DH)
                for b in range(blocks):
                    rows = pl.ds((part * blocks + b) * tokens, tokens)
                    out_ref[z, h, rows, :] = ref[b, :, columns]
    copies[2].wait()
    queries = jnp.concatenate([q_ref[i].astype(F32) for i in range(qb)], axis=0).astype(BF)
    for z in range(n_z):
        for h in range(heads):
            first = (z * heads + h) * DH
            out_ref[z, h, pl.ds(2 * blocks * tokens, qb * qt), :] = queries[:, first : first + DH]


def unpack_kernel(kv_rows, sorted_ref, kv_ref):
    n_z, heads, _, _ = sorted_ref.shape
    for h in range(heads):
        for z in range(n_z):
            for part in range(2):
                rows = sorted_ref[z, h, pl.ds(part * kv_rows, kv_rows), :]
                kv_ref[h, part, pl.ds(z * kv_rows, kv_rows), :] = rows


def spread_kernel(kv_rows, sorted_ref, q_ref):
    n_z, heads, rows, _ = sorted_ref.shape
    for h in range(heads):
        query = jnp.concatenate(
            [sorted_ref[z, h, pl.ds(2 * kv_rows, rows - 2 * kv_rows), :].astype(F32) for z in range(n_z)],
            axis=0,
        ).astype(BF)
        for to in range(q_ref.shape[0]):
            q_ref[to, h] = query


def take_kernel(first, pair_ref, out_hbm, sem):
    copy = pltpu.make_async_copy(pair_ref.at[pl.ds(first, out_hbm.shape[0])], out_hbm, sem.at[0])
    copy.start()
    copy.wait()


def block_bias(bias_ref, piece, blocks, tokens, keys):
    place = piece * blocks
    block = lax.broadcasted_iota(jnp.int32, (bias_ref.shape[0], keys), 1) // tokens % blocks
    bias = jnp.broadcast_to(bias_ref[:, place : place + 1], block.shape)
    for b in range(1, blocks):
        bias = jnp.where(block == b, bias_ref[:, place + b : place + b + 1], bias)
    return bias


def scores_of(query, key, bias):
    s = lax.dot_general(query, key, (((1,), (1,)), ((), ())), preferred_element_type=F32)
    period, keys = bias.shape
    return (s.reshape(-1, period, keys) + bias[None]).reshape(s.shape)


def weigh(scores, top, value):
    weight = jnp.exp2((scores - top) * SCALE).astype(BF)
    ones = jnp.ones(value.shape, BF)
    return jnp.dot(weight, jnp.concatenate([value, ones], axis=1), preferred_element_type=F32)


def attend_kernel(blocks, tokens, q_ref, bias_ref, *refs):
    pieces, (top_ref, total_ref, sum_ref) = refs[:-3], refs[-3:]
    n_to, heads, period, _ = q_ref.shape
    rows, keys = n_to * period, pieces[0].shape[2]
    bias = [block_bias(bias_ref, i, blocks, tokens, keys) for i in range(len(pieces))]
    for h in range(heads):
        query = q_ref[:, h].reshape(rows, DH)
        scores = [scores_of(query, ref[h, 0], item) for ref, item in zip(pieces, bias, strict=True)]
        top = jnp.max(functools.reduce(jnp.maximum, scores), axis=1, keepdims=True)
        products = [weigh(s, top, ref[h, 1]) for s, ref in zip(scores, pieces, strict=True)]
        both = functools.reduce(jnp.add, products)
        top_ref[h] = jnp.broadcast_to(top, (rows, DH))
        sum_ref[h] = both[:, :DH]
        total_ref[h] = both[:, DH:]


def last_kernel(blocks, tokens, piece, q_ref, bias_ref, low_ref, high_ref, top_ref, total_ref, sum_ref, out_ref):
    n_to, heads, period, _ = q_ref.shape
    rows, keys = n_to * period, low_ref.shape[2]
    bias = block_bias(bias_ref, piece, blocks, tokens, keys)
    lane = lax.broadcasted_iota(jnp.int32, (rows, DH), 1)
    tops = jnp.zeros((rows, DH), F32)
    totals = jnp.ones((rows, DH), F32)
    n_dest, parts, qt, _ = out_ref.shape
    qb = parts // heads
    own = qb * qt

    for h in range(heads):
        cut = low_ref.shape[0]
        pair = low_ref.at[h] if h < cut else high_ref.at[h - cut]
        scores = scores_of(q_ref[:, h].reshape(rows, DH), pair[0], bias)
        before = top_ref[h]
        top = jnp.maximum(jnp.max(scores, axis=1, keepdims=True), before)
        fade = jnp.exp2((before - top) * SCALE)
        both = weigh(scores, jnp.concatenate([top] * (keys // DH), axis=1), pair[1])
        total = total_ref[h] * fade + both[:, DH:]
        out = (sum_ref[h] * fade + both[:, :DH]) / total
        out = out.reshape(n_dest, own, DH)
        for b in range(qb):
            out_ref[:, h * qb + b] = out[:, b * qt : (b + 1) * qt].astype(BF)
        tops = jnp.where(lane == h, top, tops)
        totals = jnp.where(lane == h, total, totals)
    lse = tops * (1.0 / DH**0.5) + jnp.log(totals)
    high = lse.astype(BF).astype(F32)
    rest = lse - high
    middle = rest.astype(BF).astype(F32)
    stats = high + pltpu.roll(middle, heads, 1) + pltpu.roll(rest - middle, 2 * heads, 1)
    stats = stats.reshape(n_dest, own, DH)
    joined = stats[:, :qt]
    for b in range(1, qb):
        joined = joined + pltpu.roll(stats, b * (DH // qb), 2)[:, b * qt : (b + 1) * qt]
    out_ref[:, heads * qb] = joined.astype(BF)


def merge_kernel(n_from, part_ref, out_ref):
    n_z = part_ref.shape[0] // n_from
    qb, qt, _ = out_ref.shape
    heads = part_ref.shape[1] // qb

    stats = part_ref[:, heads * qb].astype(F32).reshape(n_from, n_z, qt, DH)
    lse = stats + pltpu.roll(stats, DH - heads, 3) + pltpu.roll(stats, DH - 2 * heads, 3)
    weight = jnp.exp(lse - jnp.max(lse, axis=0, keepdims=True))
    weight = weight / jnp.sum(weight, axis=0, keepdims=True)
    for h in range(heads):
        summed = jnp.zeros((n_z, qb * qt, DH), F32)
        for y in range(n_from):
            lanes = [b * (DH // qb) + h for b in range(qb)]
            factor = jnp.concatenate([weight[y, :, :, i : i + 1] for i in lanes], axis=1)
            out = [part_ref[pl.ds(y * n_z, n_z), h * qb + b].astype(F32) for b in range(qb)]
            summed = summed + jnp.concatenate(out, axis=1) * factor
        for z in range(n_z):
            for b in range(qb):
                rows = summed[z, b * qt : (b + 1) * qt]
                out_ref[b, :, pl.ds((z * heads + h) * DH, DH)] = rows.astype(BF)


def call(kernel, out_shape, *args, flops=0, light=False, scratch=(), space=pltpu.VMEM, out_space=pltpu.VMEM, vmem=VMEM_LIMIT):
    whole = pl.BlockSpec(memory_space=out_space)
    size = sum(a.size * a.dtype.itemsize for a in args)
    size += sum(o.size * o.dtype.itemsize for o in jax.tree.leaves(out_shape))
    if light:
        size = 0
    return pl.pallas_call(
        kernel,
        out_shape=out_shape,
        in_specs=[pl.BlockSpec(memory_space=space)] * len(args),
        out_specs=jax.tree.map(lambda _: whole, out_shape),
        scratch_shapes=list(scratch),
        compiler_params=pltpu.CompilerParams(vmem_limit_bytes=vmem),
        cost_estimate=pl.CostEstimate(flops=flops, bytes_accessed=size, transcendentals=0),
    )(*args)


def shift(block, axis, by):
    count = lax.axis_size(axis)
    return lax.ppermute(block, axis, [(i, (i + by) % count) for i in range(count)])


def local(queries, keys, values, mask_cols, mask_counts):
    n_z, n_x, n_y = lax.axis_size("head"), lax.axis_size("x"), lax.axis_size("y")
    qb, qt, d = queries.shape
    blocks, tokens, _ = keys.shape
    heads = d // n_z // DH
    kv_rows = blocks * tokens
    own = qb * qt
    period = n_z * own
    rows = n_y * period
    n_keys = n_z * kv_rows
    struct = jax.ShapeDtypeStruct

    packed = call(
        pack_kernel,
        struct((n_z, heads, 2 * kv_rows + own, DH), BF),
        queries,
        keys,
        values,
        scratch=[
            pltpu.VMEM(queries.shape, BF),
            pltpu.VMEM(keys.shape, BF),
            pltpu.VMEM(values.shape, BF),
            pltpu.SemaphoreType.DMA((3,)),
        ],
        space=pltpu.HBM, vmem=62 * 1024 * 1024,
    )
    sorted_ = lax.all_to_all(packed, "head", 0, 0)
    kv = call(
        functools.partial(unpack_kernel, kv_rows), struct((heads, 2, n_keys, DH), BF), sorted_
    )
    query = call(
        functools.partial(spread_kernel, kv_rows), struct((n_y, heads, period, DH), BF), sorted_
    )

    pair_left = shift(kv, "x", 1)
    pair_right = shift(kv, "x", -1)
    query_all = lax.all_to_all(query, "y", 0, 0, axis_index_groups=[list(range(n_y))[::-1]])
    cut = (heads + 1) // 2
    far_low, far_high = (
        shift(
            call(
                functools.partial(take_kernel, first),
                struct((count,) + kv.shape[1:], BF),
                pair,
                flops=2 * 10**10,
                scratch=[pltpu.SemaphoreType.DMA((1,))],
                out_space=pltpu.HBM,
            ),
            "x",
            by,
        )
        for pair, first, count, by in ((pair_left, 0, cut, 1), (pair_right, cut, heads - cut, -1))
    )

    x = lax.axis_index("x")
    places = jnp.stack([x, (x + n_x - 1) % n_x, (x + 1) % n_x, (x + 2) % n_x])
    owned = (places[:, None] * n_y + lax.axis_index("y")) * blocks + jnp.arange(blocks)
    owned = owned.reshape(-1)
    listed = jnp.arange(mask_cols.shape[1])[None, :] < mask_counts[:, None]
    hit = (mask_cols[:, :, None] == owned) & listed[:, :, None]
    bias = jnp.where(jnp.any(hit, axis=1), 0.0, CLOSED).astype(F32)
    bias = jnp.repeat(bias, qt, axis=0)

    flops = 4 * rows * n_keys * heads * DH
    state = call(
        functools.partial(attend_kernel, blocks, tokens),
        (struct((heads, rows, DH), F32),) * 3,
        query_all,
        bias,
        kv,
        pair_left,
        pair_right,
        light=True,
    )
    part = call(
        functools.partial(last_kernel, blocks, tokens, 3),
        struct((n_y * n_z, heads * qb + 1, qt, DH), BF),
        query_all,
        bias,
        far_low,
        far_high,
        *state,
        flops=flops,
    )
    order = [y * n_z + z for y in reversed(range(n_y)) for z in range(n_z)]
    part = lax.all_to_all(part, ("y", "head"), 0, 0, axis_index_groups=[order])
    return call(functools.partial(merge_kernel, n_y), struct((qb, qt, d), BF), part)


def solution(mesh):
    cfg, head, kv = (mesh.shape[name] for name in ("cfg", "head", "kv"))
    n_x = 4
    fine = Mesh(mesh.devices.reshape(cfg, head, n_x, kv // n_x), ("cfg", "head", "x", "y"))
    token = P(("cfg", "head"), ("x", "y"), None)
    block = P(("cfg", "x", "y"), "head", None)
    return jax.shard_map(
        local,
        mesh=fine,
        in_specs=(token, block, block, P(), P()),
        out_specs=token,
        check_vma=False,
    )
```
